256 devices in a mesh: ctx: 64 (over y, z, core), mp: 4 (over x).
Axes of the slice: x: 4, y: 4, z: 8, core: 2. Of those that a mesh axis runs over, the one named last changes fastest.
Arguments:
- hidden: bfloat16 [8192, 4096], P('ctx', 'mp'), may hold values from -6 to 6
- queries: bfloat16 [8192, 4096], P('ctx', 'mp'), may hold values from -6 to 6
- out_grad: bfloat16 [8192, 4096], P('ctx', 'mp'), may hold values from -6 to 6
- neighbours: bfloat16 [128, 4, 128, 4096], P('ctx', None, None, 'mp'), may hold values from -6 to 6
- query_gain: float32 [128], replicated, may hold values from 0.6 to 2
- key_gain: float32 [128], replicated, may hold values from 0.6 to 2
- group_counts: int32 [128], replicated, may hold values from 1 to 4, as said below
- group_owners: int32 [128], replicated, may hold values from 0 to 63, as said below
Outputs:
- attended: bfloat16 [8192, 4096], P('ctx', 'mp')
- query_grad: bfloat16 [8192, 4096], P('ctx', 'mp')
- rows_grad: bfloat16 [8192, 4096], P('ctx', 'mp')
- gain_grads: float32 [2, 128], replicated
The draws below stay inside these ranges and needn't reach their ends.
Inputs may be any that keep to these rules, and one draw needn't show every extreme that they name: `group_owners`: the owner of a group is the device that holds it or the next device along ctx (the last device hands to the first); every device hands exactly 1 of its 2 groups to the next device. `group_counts`: A group handed to the next device has at most 2 live neighbours; neighbour slots at or past a group's count are not read.
All inputs are finite; a program needn't handle non-finite values.
Results may differ from the reference program's by a relative error of at most 0.017.
Values may be sent and summed in bfloat16 or wider, within the bound.
A program may use at most 64 MiB of HBM per device.

```python
import math
import jax
import jax.numpy as jnp
from jax import lax

D = 4096
HEAD_SIZE = 128
CL = 64
NL = 128
KMAX = 4
SENT_MAX = 2
CH_DEV = 2
SENT = 1
TOKENS = 8192
GROUPS = 128


def group_plan(key):
    devices = GROUPS // CH_DEV
    order_key, kept_key, sent_key, pick_key = jax.random.split(key, 4)
    score_matrix = jax.random.randint(order_key, (devices, CH_DEV), 0, 1 << 20) * CH_DEV + jnp.arange(CH_DEV)[None, :]
    ranking = jnp.argsort(jnp.argsort(score_matrix, axis=1), axis=1)
    handed = ranking < SENT
    kept_counts = jax.random.randint(kept_key, (devices, CH_DEV), 1, KMAX + 1)
    sent_counts = jax.random.randint(sent_key, (devices, CH_DEV), 1, SENT_MAX + 1)
    chosen = jax.random.randint(pick_key, (), 0, devices)
    is_chosen = (jnp.arange(devices) == chosen)[:, None]
    sent_counts = jnp.where(is_chosen & (ranking == 0), SENT_MAX, sent_counts)
    kept_counts = jnp.where(is_chosen & (ranking == SENT), KMAX, kept_counts)
    counts = jnp.where(handed, sent_counts, kept_counts)
    holder = jnp.arange(devices)[:, None]
    owners = jnp.where(handed, (holder + 1) % devices, holder)
    return (counts.reshape(-1).astype(jnp.int32), owners.reshape(-1).astype(jnp.int32))


def draw_group_counts(key, part):
    counts, owners = group_plan(key)
    return counts


def draw_group_owners(key, part):
    counts, owners = group_plan(key)
    return owners


def shard_levels(rng, shape, pieces, smallest, largest):
    factor_of, own = 1.0, jax.random.fold_in(rng, 6)
    for axis_at, blocks in pieces:
        heights = jnp.exp(jax.random.uniform(jax.random.fold_in(own, axis_at), (blocks,), jnp.float32, smallest / len(pieces), largest / len(pieces)))
        factor_of = factor_of * jnp.repeat(heights, shape[axis_at] // blocks).reshape([-1 if axis == axis_at else 1 for axis in range(len(shape))])
    return factor_of


def bell_draw(own_key, extent, deviation, most, cuts=(), kind=jnp.bfloat16):
    factor_of = shard_levels(own_key, extent, cuts, -0.22, 0.18) if cuts else 1.0
    result = jax.random.normal(own_key, extent, jnp.float32) * deviation * factor_of
    return jnp.minimum(jnp.maximum(result, -most), most).astype(kind)


def setup_inputs(seed: int = 0) -> dict:
    key_list = jax.random.split(jax.random.key(seed), 9)
    return {
        "hidden": bell_draw(key_list[0], (TOKENS, D), 1.0, 6.0, ((0, 64), (1, 4))),
        "queries": bell_draw(key_list[1], (TOKENS, D), 1.0, 6.0, ((0, 64), (1, 4))),
        "out_grad": bell_draw(key_list[2], (TOKENS, D), 1.0, 6.0, ((0, 64), (1, 4))),
        "neighbours": bell_draw(key_list[3], (GROUPS, KMAX, NL, D), 1.0, 6.0, ((0, 64), (3, 4))),
        "query_gain": jnp.clip(jnp.exp(jax.random.uniform(key_list[4], (HEAD_SIZE,), jnp.float32, math.log(0.6), math.log(2.0))), 0.6, 2.0),
        "key_gain": jnp.clip(jnp.exp(jax.random.uniform(key_list[5], (HEAD_SIZE,), jnp.float32, math.log(0.6), math.log(2.0))), 0.6, 2.0),
        "group_counts": draw_group_counts(jax.random.fold_in(key_list[8], 71), 0),
        "group_owners": draw_group_owners(jax.random.fold_in(key_list[8], 71), 0),
    }


EPSILON = 1e-06

def to_float(value_rows):
    return lax.optimization_barrier(value_rows).astype(jnp.float32)

def head_norm(value_rows):
    shaped = value_rows.astype(jnp.float32).reshape(value_rows.shape[:-1] + (value_rows.shape[-1] // HEAD_SIZE, HEAD_SIZE))
    factor = lax.rsqrt(lax.optimization_barrier(jnp.mean(shaped * shaped, axis=-1, keepdims=True)) + EPSILON)
    return shaped * factor

def encode(neighbour_block, group_rows, query_gain, key_gain):
    slot_total, nbr_length, columns = neighbour_block.shape
    flattened = neighbour_block.reshape(slot_total * nbr_length, columns)
    encoder_query_rows = to_float((head_norm(flattened) * query_gain).astype(jnp.bfloat16))
    encoder_key_rows = to_float((head_norm(group_rows) * key_gain).astype(jnp.bfloat16))
    score_matrix = jnp.einsum('yvo,jvo->vyj', encoder_key_rows, encoder_query_rows) / math.sqrt(HEAD_SIZE)
    powered = jnp.exp(score_matrix)
    softmax_weight = to_float((powered / lax.optimization_barrier(jnp.sum(powered, axis=1, keepdims=True))).astype(jnp.bfloat16))
    value_rows = group_rows.astype(jnp.float32).reshape(group_rows.shape[0], columns // HEAD_SIZE, HEAD_SIZE)
    weighted_value_mix = jnp.einsum('rgq,gre->qre', softmax_weight, value_rows)
    encoded = flattened.astype(jnp.float32) + weighted_value_mix.reshape(slot_total * nbr_length, columns)
    return encoded.astype(jnp.bfloat16).reshape(slot_total, nbr_length, columns)

def attend(query_rows, encoded, live_count):
    slot_total, nbr_length, columns = encoded.shape
    flattened = encoded.reshape(slot_total * nbr_length, columns)
    decoder_query_rows = to_float(head_norm(query_rows).astype(jnp.bfloat16))
    decoder_key_rows = to_float(head_norm(flattened).astype(jnp.bfloat16))
    score_matrix = jnp.einsum('ybx,tbx->byt', decoder_query_rows, decoder_key_rows) / math.sqrt(HEAD_SIZE)
    live_keys = jnp.arange(slot_total * nbr_length, dtype=jnp.int32) // nbr_length < live_count
    powered = jnp.where(live_keys, jnp.exp(score_matrix), 0.0)
    softmax_weight = to_float((powered / lax.optimization_barrier(jnp.sum(powered, axis=-1, keepdims=True))).astype(jnp.bfloat16))
    value_rows = flattened.astype(jnp.float32).reshape(slot_total * nbr_length, columns // HEAD_SIZE, HEAD_SIZE)
    attention_output = jnp.einsum('tuf,ftz->utz', softmax_weight, value_rows)
    return attention_output.reshape(query_rows.shape[0], columns).astype(jnp.bfloat16)

def reference(hidden, queries, out_grad, neighbours, query_gain, key_gain, group_counts, group_owners):
    devices = GROUPS // CH_DEV
    holder = jnp.arange(GROUPS, dtype=jnp.int32) // CH_DEV
    handed = (group_owners != holder).astype(jnp.int32).reshape(devices, CH_DEV)
    kept = 1 - handed
    rank_handed = jnp.cumsum(handed, axis=1) - handed
    rank_kept = jnp.cumsum(kept, axis=1) - kept
    owner_rows = group_owners.reshape(devices, CH_DEV)
    holder_rows = holder.reshape(devices, CH_DEV)
    slot_rows = jnp.where(handed == 1, owner_rows * CH_DEV + rank_handed, holder_rows * CH_DEV + SENT + rank_kept)
    slot_rows = slot_rows.reshape(GROUPS).astype(jnp.int32)
    row_blocks = hidden.reshape(GROUPS, CL, D)
    query_blocks = queries.reshape(GROUPS, CL, D)
    grad_blocks = out_grad.reshape(GROUPS, CL, D)

    def one_group(group_id):
        neighbour_block = neighbours[slot_rows[group_id]]
        live_count = group_counts[group_id]

        def whole(query_rows, group_rows, gain_q, gain_k):
            return attend(query_rows, encode(neighbour_block, group_rows, gain_q, gain_k), live_count)
        attention_output, backward = jax.vjp(whole, query_blocks[group_id], row_blocks[group_id], query_gain, key_gain)
        grad_query, grad_rows, grad_gq, grad_gk = backward(grad_blocks[group_id])
        return (attention_output, grad_query, grad_rows, grad_gq, grad_gk)
    results = lax.map(one_group, jnp.arange(GROUPS, dtype=jnp.int32))
    attended = results[0].reshape(TOKENS, D)
    query_grad = results[1].reshape(TOKENS, D)
    rows_grad = results[2].reshape(TOKENS, D)
    gain_grads = jnp.stack([lax.optimization_barrier(jnp.sum(results[3], axis=0)), lax.optimization_barrier(jnp.sum(results[4], axis=0))])
    return (attended, query_grad, rows_grad, gain_grads)
```

```python
import functools
import math

import jax
import jax.numpy as jnp
from jax import lax
from jax.experimental import pallas as pl
from jax.experimental.pallas import tpu as pltpu
from jax.sharding import PartitionSpec as P

HEAD = 128
ROWS = 64
NBR = 128
SLOTS = 4
SENT_SLOTS = 2
EPSILON = 1e-06
SCALE = 1.0 / math.sqrt(HEAD)
LOG2E = math.log2(math.e)
MESH = pl.DeviceIdType.MESH
VMEM_LIMIT = 64 * 1024 * 1024 - 256 * 1024
BF16 = jnp.bfloat16
F32 = jnp.float32


def mm(a, b):
    return lax.dot_general(a, b, (((1,), (0,)), ((), ())), preferred_element_type=F32)


def mm_nt(a, b):
    return lax.dot_general(a, b, (((1,), (1,)), ((), ())), preferred_element_type=F32)


def mm_tn(a, b):
    return lax.dot_general(a, b, (((0,), (0,)), ((), ())), preferred_element_type=F32)


def row_norm(value):
    wide = value.astype(F32)
    factor = lax.rsqrt(jnp.mean(wide * wide, axis=1, keepdims=True) + EPSILON)
    return wide * factor, factor


def unit(x, h, q, g, gain, live, result):
    hn, rh = row_norm(h)
    qn, rq = row_norm(q)
    ek = (hn * gain).astype(BF16)
    qg = jnp.concatenate([qn.astype(BF16), g], axis=0)
    xt = jnp.transpose(x)
    xtf = xt.astype(F32)
    rx = lax.rsqrt(jnp.mean(xtf * xtf, axis=0, keepdims=True) + EPSILON)
    yield
    s = mm(ek, xt)
    yield
    p = jnp.exp2(s * (rx * (SCALE * LOG2E)))
    w = p * (1.0 / jnp.sum(p, axis=0, keepdims=True))
    wb = w.astype(BF16)
    yield
    e = xtf + mm_tn(h, wb)
    eb = e.astype(BF16)
    ef = eb.astype(F32)
    re = lax.rsqrt(jnp.mean(ef * ef, axis=0, keepdims=True) + EPSILON)
    yield
    both = mm(qg, eb)
    yield
    t, da = both[:ROWS], both[ROWS:]
    p = jnp.exp2(t * (re * (SCALE * LOG2E))) * live
    a = p * (1.0 / jnp.sum(p, axis=1, keepdims=True))
    z = a * (da - jnp.sum(a * da, axis=1, keepdims=True))
    dt = z * (re * SCALE)
    c = jnp.sum(dt * t, axis=0, keepdims=True) * (re * re * (1.0 / HEAD))
    ta = jnp.concatenate([dt.astype(BF16), a.astype(BF16)], axis=0)
    yield
    deb = (mm_tn(qg, ta) - ef * c).astype(BF16)
    yield
    dw = mm(h, deb)
    dqo = mm_nt(ta, eb)
    yield
    ds = w * (dw - jnp.sum(w * dw, axis=0, keepdims=True))
    ux = mm((ds * (rx * SCALE)).astype(BF16), x)
    dh = mm_nt(wb, deb)
    yield
    dqn = dqo[:ROWS]
    dq = rq * (dqn - qn * jnp.mean(dqn * qn, axis=1, keepdims=True))
    dhn = ux * gain
    dh = dh + rh * (dhn - hn * jnp.mean(dhn * hn, axis=1, keepdims=True))
    v = jnp.sum(ux * hn, axis=0, keepdims=True)
    result.append((dqo[ROWS:].astype(BF16), dq.astype(BF16), dh.astype(BF16), v))


def lockstep(makers):
    results = [[] for _ in makers]
    running = [make(result) for make, result in zip(makers, results)]
    while running:
        running = [r for r in running if next(r, "end") != "end"]
    return [r[0] for r in results]


def phase_near(c, m):
    pos = c % 16
    return pos, 16, lambda j: (c - pos + (pos + j) % 16, m)


def phase_far(c, m):
    pos = (c // 16) * 4 + m
    return pos, 16, lambda j: ((c % 16) + 16 * (((pos + j) % 16) // 4), (pos + j) % 4)


def main_kernel(
    heads, counts, owners, hidden, queries, out_grad, nbrs, gq, gk,
    att_out, dq_out, dh_out, v_out,
    h_buf, q_buf, g_buf, kept_buf, sent_buf, att, dq, dh, v_acc, got_near, got_far,
    in_sem, kept_sem, out_sem, send_sem, recv_sem, sum_send, sum_recv,
):
    c = lax.axis_index("ctx")
    m = lax.axis_index("mp")
    n = lax.axis_size("ctx")
    following, preceding = (c + 1) % n, (c + n - 1) % n
    phases = [phase_near(c, m), phase_far(c, m)]
    barrier = pltpu.get_barrier_semaphore()
    greeted = 0
    for d in (following, preceding):
        pl.semaphore_signal(barrier, inc=1, device_id=(d, m), device_id_type=MESH)
        greeted += 1
    for _, size, partner in phases:
        for j in range(1, size):
            pl.semaphore_signal(barrier, inc=1, device_id=partner(j), device_id_type=MESH)
            greeted += 1
    loads = [
        pltpu.make_async_copy(src, dst, in_sem.at[i])
        for i, (src, dst) in enumerate(((hidden, h_buf), (queries, q_buf), (out_grad, g_buf)))
    ]
    for load in loads:
        load.start()
    columns = heads * HEAD
    half = heads // 2
    width = half * HEAD
    kept_loads = [
        pltpu.make_async_copy(
            nbrs.at[1, :, :, pl.ds(i * width, width)], kept_buf.at[:, :, pl.ds(i * width, width)], kept_sem.at[i]
        )
        for i in range(2)
    ]
    for load in kept_loads:
        load.start()
    pl.semaphore_wait(barrier, greeted)
    sends = []
    for i in range(heads):
        cols = pl.ds(i * HEAD, HEAD)
        send = pltpu.make_async_remote_copy(
            src_ref=nbrs.at[0, pl.ds(0, SENT_SLOTS), :, cols],
            dst_ref=sent_buf.at[:, :, cols],
            send_sem=send_sem.at[i],
            recv_sem=recv_sem.at[i],
            device_id=(preceding, m),
            device_id_type=MESH,
        )
        send.start()
        sends.append(send)
    for load in loads:
        load.wait()
    for load in kept_loads:
        load.wait()
    gain = gq[...] * gk[...]
    first_kept = jnp.full((ROWS, columns), owners[2 * c], jnp.int32) == c
    lanes = lax.broadcasted_iota(jnp.int32, (1, SLOTS * NBR), 1)
    first_kept_lanes = jnp.full(lanes.shape, owners[2 * c], jnp.int32) == c
    first = jnp.full(lanes.shape, counts[2 * c] * NBR, jnp.int32)
    second = jnp.full(lanes.shape, counts[2 * c + 1] * NBR, jnp.int32)
    live = jnp.where(lanes < jnp.where(first_kept_lanes, first, second), 1.0, 0.0)
    live_sent = jnp.where(lanes < jnp.where(first_kept_lanes, second, first), 1.0, 0.0)
    live_sent = live_sent[:, : SENT_SLOTS * NBR]
    for buf in (h_buf, q_buf, g_buf):
        top, bottom = buf[:ROWS], buf[ROWS:]
        buf[:ROWS] = jnp.where(first_kept, top, bottom)
        buf[ROWS:] = jnp.where(first_kept, bottom, top)
    kept_rows, handed_rows = pl.ds(0, ROWS), pl.ds(ROWS, ROWS)
    v_acc[...] = jnp.zeros_like(v_acc)

    def work(head_list, slot, rows, nbr_buf, mask):
        makers = []
        for i in head_list:
            cols = pl.ds(pl.multiple_of(i * HEAD, HEAD), HEAD)
            x = nbr_buf[:, :, cols].reshape(-1, HEAD)
            makers.append(
                functools.partial(
                    unit, x, h_buf[rows, cols], q_buf[rows, cols], g_buf[rows, cols], gain, mask
                )
            )
        total = v_acc[...]
        for i, (o, one_dq, one_dh, v) in zip(head_list, lockstep(makers)):
            cols = pl.ds(pl.multiple_of(i * HEAD, HEAD), HEAD)
            att[slot, :, cols] = o
            dq[slot, :, cols] = one_dq
            dh[slot, :, cols] = one_dh
            total = total + v
        v_acc[...] = total

    def kept_step(i, carry):
        work([2 * i, 2 * i + 1], 0, kept_rows, kept_buf, live)
        return carry

    lax.fori_loop(0, heads // 2, kept_step, 0)
    for i in range(0, heads, 2):
        sends[i].wait_recv()
        sends[i + 1].wait_recv()
        work([i, i + 1], 1, handed_rows, sent_buf, live_sent)

    for p, (pos, size, partner) in enumerate(phases):
        got = (got_near, got_far)[p]
        for j in range(1, size):
            pltpu.make_async_remote_copy(
                src_ref=v_acc, dst_ref=got.at[pos], send_sem=sum_send.at[p], recv_sem=sum_recv.at[p],
                device_id=partner(j), device_id_type=MESH,
            ).start()
        got[pos] = v_acc[...]
        if p == 0:
            for buf, slots in ((h_buf, att), (q_buf, dq), (g_buf, dh)):
                buf[:ROWS] = jnp.where(first_kept, slots[0], slots[1])
                buf[ROWS:] = jnp.where(first_kept, slots[1], slots[0])
            stores = [
                pltpu.make_async_copy(src, dst, out_sem.at[i])
                for i, (src, dst) in enumerate(((h_buf, att_out), (q_buf, dq_out), (g_buf, dh_out)))
            ]
            for store in stores:
                store.start()
        sent = got.at[pl.ds(0, size - 1)]
        pltpu.make_async_copy(sent, sent, sum_send.at[p]).wait()
        pltpu.make_async_copy(sent, sent, sum_recv.at[p]).wait()
        v_acc[...] = jnp.sum(got[...], axis=0)
    v_out[...] = v_acc[...]
    for store in stores:
        store.wait()
    for send in sends:
        send.wait_send()


def last_kernel(att, dq, dh, v, gq, gk, att_out, dq_out, dh_out, gains_out, buf, in_sem, out_sem):
    loads = [
        pltpu.make_async_copy(src, buf.at[i], in_sem.at[i]) for i, src in enumerate((att, dq, dh))
    ]
    stores = [
        pltpu.make_async_copy(buf.at[i], dst, out_sem.at[i])
        for i, dst in enumerate((att_out, dq_out, dh_out))
    ]
    for load in loads:
        load.start()
    gains_out[0:1, :] = v[...] * gk[...]
    gains_out[1:2, :] = v[...] * gq[...]
    for load, store in zip(loads, stores):
        load.wait()
        store.start()
    for store in stores:
        store.wait()


def per_device(hidden, queries, out_grad, nbrs, query_gain, key_gain, counts, owners):
    rows, columns = hidden.shape
    heads = columns // HEAD
    block = jax.ShapeDtypeStruct((rows, columns), BF16)
    smem = pl.BlockSpec(memory_space=pltpu.SMEM)
    vmem = pl.BlockSpec(memory_space=pltpu.VMEM)
    hbm = pl.BlockSpec(memory_space=pl.ANY)
    dma = pltpu.SemaphoreType.DMA
    gq, gk = query_gain[None], key_gain[None]
    att, dq, dh, v = pl.pallas_call(
        functools.partial(main_kernel, heads),
        out_shape=[block, block, block, jax.ShapeDtypeStruct((1, HEAD), F32)],
        in_specs=[smem, smem, hbm, hbm, hbm, hbm, vmem, vmem],
        out_specs=[hbm, hbm, hbm, vmem],
        scratch_shapes=[
            *[pltpu.VMEM((rows, columns), BF16)] * 3,
            pltpu.VMEM((SLOTS, NBR, columns), BF16),
            pltpu.VMEM((SENT_SLOTS, NBR, columns), BF16),
            *[pltpu.VMEM((2, ROWS, columns), BF16)] * 3,
            pltpu.VMEM((1, HEAD), F32),
            pltpu.VMEM((16, 1, HEAD), F32),
            pltpu.VMEM((16, 1, HEAD), F32),
            dma((3,)), dma((2,)), dma((3,)), dma((heads,)), dma((heads,)), dma((2,)), dma((2,)),
        ],
        compiler_params=pltpu.CompilerParams(
            collective_id=0, has_side_effects=True, vmem_limit_bytes=VMEM_LIMIT
        ),
    )(counts, owners, hidden, queries, out_grad, nbrs, gq, gk)
    return pl.pallas_call(
        last_kernel,
        out_shape=[block, block, block, jax.ShapeDtypeStruct((2, HEAD), F32)],
        in_specs=[hbm, hbm, hbm, vmem, vmem, vmem],
        out_specs=[hbm, hbm, hbm, vmem],
        scratch_shapes=[pltpu.VMEM((3, rows, columns), BF16), dma((3,)), dma((3,))],
        compiler_params=pltpu.CompilerParams(vmem_limit_bytes=VMEM_LIMIT),
    )(att, dq, dh, v, gq, gk)


def solution(mesh):
    in_specs = (
        P("ctx", "mp"),
        P("ctx", "mp"),
        P("ctx", "mp"),
        P("ctx", None, None, "mp"),
        P(),
        P(),
        P(),
        P(),
    )
    out_specs = (P("ctx", "mp"), P("ctx", "mp"), P("ctx", "mp"), P())
    return jax.shard_map(
        per_device, mesh=mesh, in_specs=in_specs, out_specs=out_specs, check_vma=False
    )
```

```python
import functools
import math

import jax
import jax.numpy as jnp
from jax import lax
from jax.experimental import pallas as pl
from jax.experimental.pallas import tpu as pltpu
from jax.sharding import PartitionSpec as P

HEAD = 128
ROWS = 64
NBR = 128
SLOTS = 4
SENT_SLOTS = 2
PAIR = 2 * HEAD
EPSILON = 1e-06
SCALE = 1.0 / math.sqrt(HEAD)
LOG2E = math.log2(math.e)
MESH = pl.DeviceIdType.MESH
VMEM_LIMIT = 63 * 1024 * 1024
BF16 = jnp.bfloat16
F32 = jnp.float32


def mm(a, b):
    return lax.dot_general(a, b, (((1,), (0,)), ((), ())), preferred_element_type=F32)


def mm_nt(a, b):
    return lax.dot_general(a, b, (((1,), (1,)), ((), ())), preferred_element_type=F32)


def mm_tn(a, b):
    return lax.dot_general(a, b, (((0,), (0,)), ((), ())), preferred_element_type=F32)


def row_norm(value):
    wide = value.astype(F32)
    factor = lax.rsqrt(jnp.mean(wide * wide, axis=1, keepdims=True) + EPSILON)
    return wide * factor, factor


def over_rows(value, row):
    k = row.shape[0]
    return (value.reshape(-1, k, value.shape[1]) * row[None]).reshape(value.shape)


def unit(x, h, q, g, gain, live, result):
    eye = (
        lax.broadcasted_iota(jnp.int32, (HEAD, HEAD), 0)
        == lax.broadcasted_iota(jnp.int32, (HEAD, HEAD), 1)
    ).astype(BF16)
    ones = jnp.ones((16, HEAD), BF16)
    root = math.sqrt(HEAD)
    xt = jnp.transpose(x)
    hf, qf = h.astype(F32), q.astype(F32)
    rh = lax.rsqrt(jnp.sum(hf * hf, axis=1, keepdims=True) + HEAD * EPSILON)
    rq = lax.rsqrt(jnp.sum(qf * qf, axis=1, keepdims=True) + HEAD * EPSILON)
    hn, qn = hf * rh, qf * rq
    ek = (hn * gain).astype(BF16)
    qg = jnp.concatenate([qn.astype(BF16), g], axis=0)
    rx = lax.rsqrt(mm(ones, xt * xt) + HEAD * EPSILON)
    yield
    s = mm(ek, xt)
    yield
    p = jnp.exp2(over_rows(s, rx[:8] * (root * LOG2E)))
    wb = (p * (1.0 / jnp.sum(p, axis=0, keepdims=True))).astype(BF16)
    yield
    eb = mm(jnp.concatenate([eye, jnp.transpose(h)], axis=1), jnp.concatenate([xt, wb], axis=0)).astype(BF16)
    yield
    both = mm(qg, eb)
    re = lax.rsqrt(mm(ones, eb * eb) + HEAD * EPSILON)
    yield
    t, da = both[:ROWS], both[ROWS:]
    p = jnp.exp2(over_rows(t, re[:8] * (root * LOG2E)))
    p = jnp.concatenate([p[:, :NBR], p[:, NBR:] * live[:, NBR:]], axis=1)
    inv = 1.0 / jnp.sum(p, axis=1, keepdims=True)
    shift = jnp.sum(p * da, axis=1, keepdims=True) * inv
    ab = (p * inv).astype(BF16)
    dt = over_rows(ab * (da - shift).astype(BF16), (re * root).astype(BF16))
    ta = jnp.concatenate([dt, ab], axis=0)
    yield
    c = mm(ones[:, :ROWS], dt * t.astype(BF16)) * (re * re)
    ec = over_rows(eb, (-c).astype(BF16))
    yield
    deb = mm(jnp.concatenate([jnp.transpose(qg), eye], axis=1), jnp.concatenate([ta, ec], axis=0)).astype(BF16)
    yield
    dw = mm(h, deb)
    yield
    dk = mm(ones[:, :ROWS], wb * dw.astype(BF16))
    ds = wb * (dw.reshape(-1, 8, dw.shape[1]) - dk[None, :8]).reshape(dw.shape).astype(BF16)
    yield
    ux = mm(over_rows(ds, (rx * root).astype(BF16)), x)
    yield
    u = ux * hn
    result.append(jnp.sum(u, axis=0, keepdims=True))
    yield "v"
    dqo = mm_nt(ta, eb)
    dh = mm_nt(wb, deb)
    yield
    dqn = dqo[:ROWS]
    dq = rq * (dqn - qn * jnp.sum(dqn * qn, axis=1, keepdims=True))
    dh = dh + rh * (ux * gain - hn * jnp.sum(u * gain, axis=1, keepdims=True))
    result.append((dqo[ROWS:].astype(BF16), dq.astype(BF16), dh.astype(BF16)))


def staggered(waiting, every, finish, later, at_once=1):
    waiting, running, tick = list(waiting), [], 0
    while waiting or running:
        if tick % every == 0:
            running, waiting = running + waiting[:at_once], waiting[at_once:]
        still = []
        for number, steps in running:
            if not hasattr(steps, "send"):
                steps = steps()
            mark = next(steps, "end")
            if mark == "end":
                finish(number)
            elif mark == "v" and later(number):
                continue
            else:
                still.append((number, steps))
        running = still
        tick += 1


def main_kernel(
    heads, counts_in, owners_in, hidden, queries, out_grad, nbrs, gq_in, gk_in,
    att_out, dq_out, dh_out, gains_out,
    counts, owners, gq, gk, rows_buf, kept_buf, sent_buf, stage, guest, guest_out, back, done, v_acc, total, got_line, got_plane,
    small_sem, in_sem, kept_sem, own_sem, send_sem, recv_sem, guest_send, guest_recv, back_send, back_recv, sum_send, sum_recv,
):
    c = lax.axis_index("ctx")
    m = lax.axis_index("mp")
    n = lax.axis_size("ctx")
    following, preceding = lax.rem(c + 1, n), lax.rem(c + n - 1, n)
    core, z, y = lax.rem(c, 2), lax.rem(lax.div(c, 2), 8), lax.div(c, 16)
    odd = core == 1
    columns = heads * HEAD
    moved = heads // 2
    pairs = (heads - moved) // 2

    line_at = [y * 16 + lax.rem(z + j, 8) * 2 for j in range(8)]
    y_at = [lax.rem(y + j, 4) * 16 + z * 2 for j in range(4)]
    m_at = [lax.rem(m + j, 4) for j in range(4)]

    def line(j, other):
        return (line_at[j] + other, m)

    def plane(j, other):
        return (y_at[j // 4] + other, m_at[j % 4])

    barrier = pltpu.get_barrier_semaphore()

    def greet(device):
        pl.semaphore_signal(barrier, inc=1, device_id=device, device_id_type=MESH)

    @pl.when(odd)
    def _():
        for j in (4, 3, 5, 2, 6, 1, 7):
            greet(line(j, 0))
            greet(line(j, 1))

    for j in (10, 6, 9, 11, 14, 2, 8, 5, 7, 13, 15, 1, 3, 4, 12):
        greet(plane(j, 1))
    greet((following, m))
    greet((preceding, m))
    greet((c + 1 - 2 * core, m))

    small = [
        pltpu.make_async_copy(src, dst, small_sem.at[i])
        for i, (src, dst) in enumerate(((owners_in, owners), (counts_in, counts), (gq_in, gq), (gk_in, gk)))
    ]
    for load in small:
        load.start()
    loads = [
        pltpu.make_async_copy(src, rows_buf.at[i], in_sem.at[i])
        for i, src in enumerate((hidden, queries, out_grad))
    ]
    for load in loads:
        load.start()
    half = columns // 2
    kept_loads = [
        pltpu.make_async_copy(
            nbrs.at[1, :, :, pl.ds(i * half, half)], kept_buf.at[:, :, pl.ds(i * half, half)], kept_sem.at[i]
        )
        for i in range(2)
    ]
    own_cols = pl.ds(moved * HEAD, columns - moved * HEAD)
    own_load = pltpu.make_async_copy(
        nbrs.at[0, pl.ds(0, SENT_SLOTS), :, own_cols], sent_buf.at[:, :, own_cols], own_sem
    )
    for load in kept_loads:
        load.start()

    own_load.start()
    for load in small:
        load.wait()
    gain = gq[...] * gk[...]
    lanes = lax.broadcasted_iota(jnp.int32, (1, SLOTS * NBR), 1)

    def masks(device):
        first_kept = jnp.full(lanes.shape, owners[2 * device], jnp.int32) == device
        first = jnp.full(lanes.shape, counts[2 * device] * NBR, jnp.int32)
        second = jnp.full(lanes.shape, counts[2 * device + 1] * NBR, jnp.int32)
        kept = jnp.where(lanes < jnp.where(first_kept, first, second), 1.0, 0.0)
        handed = jnp.where(lanes < jnp.where(first_kept, second, first), 1.0, 0.0)
        return kept, handed[:, : SENT_SLOTS * NBR]

    live, live_sent = masks(c)
    live_guest = masks(preceding)[1]
    for load in loads:
        load.wait()
    first_kept = jnp.full((ROWS, columns), owners[2 * c], jnp.int32) == c
    for k in range(3):
        top, bottom = rows_buf[k, :ROWS], rows_buf[k, ROWS:]
        rows_buf[k, :ROWS] = jnp.where(first_kept, top, bottom)
        handed = jnp.where(first_kept, bottom, top)
        rows_buf[k, ROWS:] = handed
        for p in range(pairs):
            at = moved * HEAD + p * PAIR
            stage[p, k] = handed[:, at : at + PAIR]
    for load in kept_loads:
        load.wait()

    sends = [
        pltpu.make_async_remote_copy(
            src_ref=nbrs.at[0, pl.ds(0, SENT_SLOTS), :, pl.ds(i * HEAD, HEAD)],
            dst_ref=sent_buf.at[:, :, pl.ds(i * HEAD, HEAD)],
            send_sem=send_sem.at[i], recv_sem=recv_sem.at[i],
            device_id=(preceding, m), device_id_type=MESH,
        )
        for i in range(moved)
    ]
    guests = [
        pltpu.make_async_remote_copy(
            src_ref=stage.at[p], dst_ref=guest.at[p], send_sem=guest_send.at[p], recv_sem=guest_recv.at[p],
            device_id=(following, m), device_id_type=MESH,
        )
        for p in range(pairs)
    ]
    backs = [
        pltpu.make_async_remote_copy(
            src_ref=guest_out.at[p], dst_ref=back.at[p], send_sem=back_send.at[p], recv_sem=back_recv.at[p],
            device_id=(preceding, m), device_id_type=MESH,
        )
        for p in range(pairs)
    ]

    def exchange():
        @pl.when(odd)
        def _():
            pl.semaphore_wait(barrier, 2 + 7 + 31)

        @pl.when(jnp.logical_not(odd))
        def _():
            pl.semaphore_wait(barrier, 2 + 8)

        for p in range(pairs):
            guests[p].start()
            for i in range(p * moved // pairs, (p + 1) * moved // pairs):
                sends[i].start()

    def kept_unit(i, result):
        if i == 0:
            exchange()
        cols = pl.ds(i * HEAD, HEAD)
        rows = [rows_buf[k, :ROWS, cols] for k in range(3)]
        return unit(kept_buf[:, :, cols].reshape(-1, HEAD), *rows, gain, live, result)

    def sent_unit(i, result):
        if 2 == 0:
            sends[i].wait_recv()
        elif i % 2 == 0:
            for k in range(i, i + 2):
                sends[k].wait_recv()
        cols = pl.ds(i * HEAD, HEAD)
        rows = [rows_buf[k, ROWS:, cols] for k in range(3)]
        return unit(sent_buf[:, :, cols].reshape(-1, HEAD), *rows, gain, live_sent, result)

    def guest_unit(i, result):
        p, r = divmod(i - moved, 2)
        if i == moved:
            own_load.wait()
        if 2 == 0 and r == 0:
            guests[p].wait_recv()
        elif 2 and i == moved:
            for k in range(pairs):
                guests[k].wait_recv()
        cols = pl.ds(i * HEAD, HEAD)
        rows = [guest[p, k, :, r * HEAD : (r + 1) * HEAD] for k in range(3)]
        return unit(sent_buf[:, :, cols].reshape(-1, HEAD), *rows, gain, live_guest, result)

    order = [(0, i) for i in range(heads)]
    order += [(2, i) for i in range(moved, heads)] + [(1, i) for i in range(moved)]
    results = [[] for _ in order]
    parked = []

    def open_unit(number):
        kind, i = order[number]
        return (kept_unit, sent_unit, guest_unit)[kind](i, results[number])

    makers = [(number, functools.partial(open_unit, number)) for number in range(len(order))]

    def finish(number):
        kind, i = order[number]
        for k in range(3):
            value = results[number][1][k]
            if kind == 2:
                p, r = divmod(i - moved, 2)
                guest_out[p, k, :, r * HEAD : (r + 1) * HEAD] = value
            else:
                done[kind, k, :, pl.ds(i * HEAD, HEAD)] = value
        if kind == 2 and r == 1:
            backs[p].start()

    def later(number):
        wait = True
        if wait:
            parked.append(number)
        return wait

    opened = {}

    def begin(number):
        opened[number] = open_unit(number)
        return opened[number]

    makers = [(number, functools.partial(begin, number)) for number in range(len(order))]
    staggered(makers[:heads], 1, finish, lambda number: False, 2)
    staggered(makers[heads:], 1, finish, later, 2)
    v_acc[...] = sum(result[0] for result in results)

    def give(src, slot, phase, device):
        pltpu.make_async_remote_copy(
            src_ref=src, dst_ref=slot, send_sem=sum_send.at[phase], recv_sem=sum_recv.at[phase],
            device_id=device, device_id_type=MESH,
        ).start()

    def settle(ref, sem):
        pltpu.make_async_copy(ref, ref, sem).wait()

    in_line, in_plane = z * 2 + core, y * 4 + m
    for j in range(1, 8):
        give(v_acc, got_line.at[in_line], 0, line(j, 1))

    @pl.when(jnp.logical_not(odd))
    def _():
        give(v_acc, got_line.at[in_line], 0, (c + 1, m))

    staggered([(number, opened[number]) for number in parked], 1, finish, lambda number: False)

    @pl.when(odd)
    def _():
        got_line[in_line] = v_acc[...]
        settle(got_line.at[pl.ds(0, 15)], sum_recv.at[0])
        total[...] = jnp.sum(got_line[...], axis=0)
        for j in range(1, 16):
            give(total, got_plane.at[in_plane], 1, plane(j, 1))
            give(total, got_plane.at[in_plane], 1, plane(j, 0))
        give(total, got_plane.at[in_plane], 1, (c - 1, m))
        got_plane[in_plane] = total[...]


    for copy in backs:
        copy.wait_recv()
    for k, out in enumerate((att_out, dq_out, dh_out)):
        for at in range(0, columns, PAIR):
            cols = slice(at, at + PAIR)
            kept = done[0, k, :, cols]
            handed = done[1, k, :, cols] if at < moved * HEAD else back[(at - moved * HEAD) // PAIR, k]
            out[:ROWS, cols] = jnp.where(first_kept[:, cols], kept, handed)
            out[ROWS:, cols] = jnp.where(first_kept[:, cols], handed, kept)
    for copy in sends + guests + backs:
        copy.wait_send()

    @pl.when(odd)
    def _():
        settle(got_line.at[pl.ds(0, 7)], sum_send.at[0])
        settle(got_plane.at[pl.ds(0, 15)], sum_recv.at[1])
        settle(got_plane.at[pl.ds(0, 15)], sum_send.at[1])
        settle(got_plane, sum_send.at[1])

    @pl.when(jnp.logical_not(odd))
    def _():
        settle(got_line.at[pl.ds(0, 8)], sum_send.at[0])
        settle(got_plane, sum_recv.at[1])

    v = jnp.sum(got_plane[...], axis=0)
    gains_out[0:1, :] = v * gk[...]
    gains_out[1:2, :] = v * gq[...]


def last_kernel(*refs):
    sources, targets, sem = refs[:4], refs[4:8], refs[8]
    stores = [
        pltpu.make_async_copy(src, dst, sem.at[i]) for i, (src, dst) in enumerate(zip(sources, targets))
    ]
    for store in stores:
        store.start()
    for store in stores:
        store.wait()


def per_device(hidden, queries, out_grad, nbrs, query_gain, key_gain, counts, owners):
    rows, columns = hidden.shape
    heads = columns // HEAD
    block = jax.ShapeDtypeStruct((rows, columns), BF16)
    vmem = pl.BlockSpec(memory_space=pltpu.VMEM)
    hbm = pl.BlockSpec(memory_space=pl.ANY)
    dma = pltpu.SemaphoreType.DMA
    gq, gk = query_gain[None], key_gain[None]
    moved = heads // 2
    pairs = (heads - moved) // 2
    results = pl.pallas_call(
        functools.partial(main_kernel, heads),
        out_shape=[pltpu.VMEM((rows, columns), BF16)] * 3 + [pltpu.VMEM((2, HEAD), F32)],
        in_specs=[hbm] * 8,
        out_specs=[vmem, vmem, vmem, vmem],
        scratch_shapes=[
            pltpu.SMEM(counts.shape, jnp.int32),
            pltpu.SMEM(counts.shape, jnp.int32),
            pltpu.VMEM((1, HEAD), F32),
            pltpu.VMEM((1, HEAD), F32),
            pltpu.VMEM((3, rows, columns), BF16),
            pltpu.VMEM((SLOTS, NBR, columns), BF16),
            pltpu.VMEM((SENT_SLOTS, NBR, columns), BF16),
            *[pltpu.VMEM((pairs, 3, ROWS, PAIR), BF16)] * 4,
            pltpu.VMEM((2, 3, ROWS, columns), BF16),
            pltpu.VMEM((1, HEAD), F32),
            pltpu.VMEM((1, HEAD), F32),
            pltpu.VMEM((16, 1, HEAD), F32),
            pltpu.VMEM((16, 1, HEAD), F32),
            dma((4,)), dma((3,)), dma((2,)), dma, dma((moved,)), dma((moved,)), dma((pairs,)), dma((pairs,)),
            dma((pairs,)), dma((pairs,)), dma((2,)), dma((2,)),
        ],
        compiler_params=pltpu.CompilerParams(
            collective_id=0, has_side_effects=True, vmem_limit_bytes=VMEM_LIMIT
        ),
    )(counts, owners, hidden, queries, out_grad, nbrs, gq, gk)
    return pl.pallas_call(
        last_kernel,
        out_shape=[block, block, block, jax.ShapeDtypeStruct((2, HEAD), F32)],
        in_specs=[vmem] * 4,
        out_specs=[hbm] * 4,
        scratch_shapes=[dma((4,))],
        compiler_params=pltpu.CompilerParams(vmem_limit_bytes=8 * 1024 * 1024),
    )(*results)


def solution(mesh):
    in_specs = (
        P("ctx", "mp"),
        P("ctx", "mp"),
        P("ctx", "mp"),
        P("ctx", None, None, "mp"),
        P(),
        P(),
        P(),
        P(),
    )
    out_specs = (P("ctx", "mp"), P("ctx", "mp"), P("ctx", "mp"), P())
    return jax.shard_map(
        per_device, mesh=mesh, in_specs=in_specs, out_specs=out_specs, check_vma=False
    )
```

```python
import functools
import math

import jax
import jax.numpy as jnp
from jax import lax
from jax.experimental import pallas as pl
from jax.experimental.pallas import tpu as pltpu
from jax.sharding import PartitionSpec as P

HEAD = 128
ROWS = 64
NBR = 128
SLOTS = 4
SENT_SLOTS = 2
PAIR = 2 * HEAD
EPSILON = 1e-06
SCALE = 1.0 / math.sqrt(HEAD)
LOG2E = math.log2(math.e)
FAR_FIRST = (10, 6, 9, 11, 14, 2, 8, 5, 7, 13, 15, 1, 3, 4, 12)
MESH = pl.DeviceIdType.MESH
VMEM_LIMIT = 63 * 1024 * 1024
BF16 = jnp.bfloat16
F32 = jnp.float32


def mm(a, b):
    return lax.dot_general(a, b, (((1,), (0,)), ((), ())), preferred_element_type=F32)


def mm_nt(a, b):
    return lax.dot_general(a, b, (((1,), (1,)), ((), ())), preferred_element_type=F32)


def mm_tn(a, b):
    return lax.dot_general(a, b, (((0,), (0,)), ((), ())), preferred_element_type=F32)


def row_norm(value):
    wide = value.astype(F32)
    factor = lax.rsqrt(jnp.mean(wide * wide, axis=1, keepdims=True) + EPSILON)
    return wide * factor, factor


def over_rows(value, row):
    k = row.shape[0]
    return (value.reshape(-1, k, value.shape[1]) * row[None]).reshape(value.shape)


def unit(get_x, get_rows, x_first, gain, live, result):
    eye = (
        lax.broadcasted_iota(jnp.int32, (HEAD, HEAD), 0)
        == lax.broadcasted_iota(jnp.int32, (HEAD, HEAD), 1)
    ).astype(BF16)
    ones = jnp.ones((16, HEAD), BF16)
    root = math.sqrt(HEAD)

    def from_x(x):
        xt = jnp.transpose(x)
        return x, xt, lax.rsqrt(mm(ones, xt * xt) + HEAD * EPSILON)

    def from_rows(h, q, g):
        hf, qf = h.astype(F32), q.astype(F32)
        rh = lax.rsqrt(jnp.sum(hf * hf, axis=1, keepdims=True) + HEAD * EPSILON)
        rq = lax.rsqrt(jnp.sum(qf * qf, axis=1, keepdims=True) + HEAD * EPSILON)
        hn, qn = hf * rh, qf * rq
        qg = jnp.concatenate([qn.astype(BF16), g], axis=0)
        mix = jnp.concatenate([eye, jnp.transpose(h)], axis=1)
        back_mix = jnp.concatenate([jnp.transpose(qg), eye], axis=1)
        return h, rh, rq, hn, qn, qg, mix, back_mix, (hn * gain).astype(BF16)

    if x_first:
        x, xt, rx = from_x(get_x())
        yield "pre"
        h, rh, rq, hn, qn, qg, mix, back_mix, ek = from_rows(*get_rows())
    else:
        h, rh, rq, hn, qn, qg, mix, back_mix, ek = from_rows(*get_rows())
        yield "pre"
        x, xt, rx = from_x(get_x())
    yield
    s = mm(ek, xt)
    yield
    p = jnp.exp2(over_rows(s, rx[:8] * (root * LOG2E)))
    wb = (p * (1.0 / jnp.sum(p, axis=0, keepdims=True))).astype(BF16)
    yield
    eb = mm(mix, jnp.concatenate([xt, wb], axis=0)).astype(BF16)
    yield
    both = mm(qg, eb)
    re = lax.rsqrt(mm(ones, eb * eb) + HEAD * EPSILON)
    yield
    t, da = both[:ROWS], both[ROWS:]
    p = jnp.exp2(over_rows(t, re[:8] * (root * LOG2E)))
    p = jnp.concatenate([p[:, :NBR], p[:, NBR:] * live[:, NBR:]], axis=1)
    inv = 1.0 / jnp.sum(p, axis=1, keepdims=True)
    shift = jnp.sum(p * da, axis=1, keepdims=True) * inv
    ab = (p * inv).astype(BF16)
    dtf = over_rows(p * inv * (da - shift), re[:8] * root)
    dt = dtf.astype(BF16)
    ta = jnp.concatenate([dt, ab], axis=0)
    yield
    c = jnp.sum(dtf * t, axis=0, keepdims=True) * (re * re)
    ec = over_rows(eb, (-c).astype(BF16))
    yield
    deb = mm(back_mix, jnp.concatenate([ta, ec], axis=0)).astype(BF16)
    yield
    dw = mm(h, deb)
    yield
    ds = wb * (dw - jnp.sum(wb.astype(F32) * dw, axis=0, keepdims=True)).astype(BF16)
    ux = mm(over_rows(ds, (rx * root).astype(BF16)), x)
    yield
    u = ux * hn
    result.append(jnp.sum(u, axis=0, keepdims=True))
    yield "v"
    dqo = mm_nt(ta, eb)
    dh = mm_nt(wb, deb)
    yield
    dqn = dqo[:ROWS]
    dq = rq * (dqn - qn * jnp.sum(dqn * qn, axis=1, keepdims=True))
    dh = dh + rh * (ux * gain - hn * jnp.sum(u * gain, axis=1, keepdims=True))
    result.append((dqo[ROWS:].astype(BF16), dq.astype(BF16), dh.astype(BF16)))


def staggered(waiting, every, finish, later, at_once=1):
    waiting, running, tick = list(waiting), [], 0
    while waiting or running:
        if tick % every == 0:
            running, waiting = running + waiting[:at_once], waiting[at_once:]
        still = []
        for number, steps in running:
            if not hasattr(steps, "send"):
                steps = steps()
            mark = next(steps, "end")
            if mark == "end":
                finish(number)
            elif mark in ("pre", "v") and later(number, mark):
                continue
            else:
                still.append((number, steps))
        running = still
        tick += 1


def main_kernel(
    heads, counts_in, owners_in, hidden, queries, out_grad, nbrs, gq_in, gk_in,
    att_out, dq_out, dh_out, gains_out,
    counts, owners, gq, gk, rows_buf, kept_buf, sent_buf, stage, guest, guest_out, back, done, v_acc, total, got_line, got_plane,
    small_sem, in_sem, kept_sem, own_sem, send_sem, recv_sem, guest_send, guest_recv, back_send, back_recv, sum_send, sum_recv,
):
    c = lax.axis_index("ctx")
    m = lax.axis_index("mp")
    n = lax.axis_size("ctx")
    following, preceding = lax.rem(c + 1, n), lax.rem(c + n - 1, n)
    core, z, y = lax.rem(c, 2), lax.rem(lax.div(c, 2), 8), lax.div(c, 16)
    odd = core == 1
    columns = heads * HEAD
    moved = heads // 2
    pairs = (heads - moved) // 2

    line_at = [y * 16 + lax.rem(z + j, 8) * 2 for j in range(8)]
    y_at = [lax.rem(y + j, 4) * 16 + z * 2 for j in range(4)]
    m_at = [lax.rem(m + j, 4) for j in range(4)]

    def line(j, other):
        return (line_at[j] + other, m)

    def plane(j, other):
        return (y_at[j // 4] + other, m_at[j % 4])

    barrier = pltpu.get_barrier_semaphore()

    def greet(device):
        pl.semaphore_signal(barrier, inc=1, device_id=device, device_id_type=MESH)

    @pl.when(odd)
    def _():
        for j in (4, 3, 5, 2, 6, 1, 7):
            greet(line(j, 0))
            greet(line(j, 1))

    for j in FAR_FIRST:
        greet(plane(j, 1))
    greet((following, m))
    greet((preceding, m))
    greet((c + 1 - 2 * core, m))

    small = [
        pltpu.make_async_copy(src, dst, small_sem.at[i])
        for i, (src, dst) in enumerate(((owners_in, owners), (counts_in, counts), (gq_in, gq), (gk_in, gk)))
    ]
    for load in small:
        load.start()
    loads = [
        pltpu.make_async_copy(src, rows_buf.at[i], in_sem.at[i])
        for i, src in enumerate((hidden, queries, out_grad))
    ]
    for load in loads:
        load.start()
    half = columns // 2
    kept_loads = [
        pltpu.make_async_copy(
            nbrs.at[1, :, :, pl.ds(i * half, half)], kept_buf.at[:, :, pl.ds(i * half, half)], kept_sem.at[i]
        )
        for i in range(2)
    ]
    own_cols = pl.ds(moved * HEAD, columns - moved * HEAD)
    own_load = pltpu.make_async_copy(
        nbrs.at[0, pl.ds(0, SENT_SLOTS), :, own_cols], sent_buf.at[:, :, own_cols], own_sem
    )
    for load in kept_loads:
        load.start()

    own_load.start()
    for load in small:
        load.wait()
    gain = gq[...] * gk[...]
    lanes = lax.broadcasted_iota(jnp.int32, (1, SLOTS * NBR), 1)

    def masks(device):
        first_kept = jnp.full(lanes.shape, owners[2 * device], jnp.int32) == device
        first = jnp.full(lanes.shape, counts[2 * device] * NBR, jnp.int32)
        second = jnp.full(lanes.shape, counts[2 * device + 1] * NBR, jnp.int32)
        kept = jnp.where(lanes < jnp.where(first_kept, first, second), 1.0, 0.0)
        handed = jnp.where(lanes < jnp.where(first_kept, second, first), 1.0, 0.0)
        return kept, handed[:, : SENT_SLOTS * NBR]

    live, live_sent = masks(c)
    live_guest = masks(preceding)[1]
    for load in loads:
        load.wait()
    first_kept = jnp.full((ROWS, columns), owners[2 * c], jnp.int32) == c
    for k in range(3):
        top, bottom = rows_buf[k, :ROWS], rows_buf[k, ROWS:]
        rows_buf[k, :ROWS] = jnp.where(first_kept, top, bottom)
        handed = jnp.where(first_kept, bottom, top)
        rows_buf[k, ROWS:] = handed
        for p in range(pairs):
            at = moved * HEAD + p * PAIR
            stage[p, k] = handed[:, at : at + PAIR]
    @pl.when(odd)
    def _():
        pl.semaphore_wait(barrier, 2 + 7 + 31)

    @pl.when(jnp.logical_not(odd))
    def _():
        pl.semaphore_wait(barrier, 2 + 8)

    sends = [
        pltpu.make_async_remote_copy(
            src_ref=nbrs.at[0, pl.ds(0, SENT_SLOTS), :, pl.ds(i * HEAD, HEAD)],
            dst_ref=sent_buf.at[:, :, pl.ds(i * HEAD, HEAD)],
            send_sem=send_sem.at[i], recv_sem=recv_sem.at[i],
            device_id=(preceding, m), device_id_type=MESH,
        )
        for i in range(moved)
    ]
    for copy in sends:
        copy.start()
    guests = [
        pltpu.make_async_remote_copy(
            src_ref=stage.at[p], dst_ref=guest.at[p], send_sem=guest_send.at[p], recv_sem=guest_recv.at[p],
            device_id=(following, m), device_id_type=MESH,
        )
        for p in range(pairs)
    ]
    backs = [
        pltpu.make_async_remote_copy(
            src_ref=guest_out.at[p], dst_ref=back.at[p], send_sem=back_send.at[p], recv_sem=back_recv.at[p],
            device_id=(preceding, m), device_id_type=MESH,
        )
        for p in range(pairs)
    ]

    for copy in guests:
        copy.start()
    for load in kept_loads:
        load.wait()


    def block(buf, i):
        return buf[:, :, pl.ds(i * HEAD, HEAD)].reshape(-1, HEAD)

    def own_rows(first, i):
        return [rows_buf[k, first : first + ROWS, pl.ds(i * HEAD, HEAD)] for k in range(3)]

    def kept_unit(i, result):
        return unit(lambda: block(kept_buf, i), lambda: own_rows(0, i), False, gain, live, result)

    def sent_unit(i, result):
        def arrived():
            if i % 2 == 0:
                sends[i].wait_recv()
                sends[i + 1].wait_recv()
            return block(sent_buf, i)

        return unit(arrived, lambda: own_rows(ROWS, i), False, gain, live_sent, result)

    def guest_unit(i, result):
        p, r = divmod(i - moved, 2)

        def arrived():
            if r == 0:
                guests[p].wait_recv()
            return [guest[p, k, :, r * HEAD : (r + 1) * HEAD] for k in range(3)]

        return unit(lambda: block(sent_buf, i), arrived, True, gain, live_guest, result)

    order = [(0, i) for i in range(heads)]
    for p in range(pairs):
        order += [(1, 2 * p), (1, 2 * p + 1), (2, moved + 2 * p), (2, moved + 2 * p + 1)]
    results = [[] for _ in order]
    parked = []

    def open_unit(number):
        kind, i = order[number]
        return (kept_unit, sent_unit, guest_unit)[kind](i, results[number])

    makers = [(number, functools.partial(open_unit, number)) for number in range(len(order))]

    def finish(number):
        kind, i = order[number]
        for k in range(3):
            value = results[number][1][k]
            if kind == 2:
                p, r = divmod(i - moved, 2)
                guest_out[p, k, :, r * HEAD : (r + 1) * HEAD] = value
            else:
                done[kind, k, :, pl.ds(i * HEAD, HEAD)] = value
        if kind == 2 and r == 1:
            backs[p].start()

    opened = {}

    def begin(number):
        opened[number] = open_unit(number)
        return opened[number]

    makers = [(number, functools.partial(begin, number)) for number in range(len(order))]
    ready = []

    def hold(number, mark):
        held = number >= heads and mark == "pre"
        if held:
            ready.append((number, opened[number]))
        return held

    def park(number, mark):
        if mark == "v":
            parked.append(number)
        return mark == "v"

    own_load.wait()
    staggered(makers, 1, finish, hold, 2)
    staggered(ready, 1, finish, park, 2)
    v_acc[...] = sum(result[0] for result in results)

    def give(src, slot, phase, device):
        pltpu.make_async_remote_copy(
            src_ref=src, dst_ref=slot, send_sem=sum_send.at[phase], recv_sem=sum_recv.at[phase],
            device_id=device, device_id_type=MESH,
        ).start()

    def settle(ref, sem):
        pltpu.make_async_copy(ref, ref, sem).wait()

    in_line, in_plane = z * 2 + core, y * 4 + m
    for j in (4, 3, 5, 2, 6, 1, 7):
        give(v_acc, got_line.at[in_line], 0, line(j, 1))

    @pl.when(jnp.logical_not(odd))
    def _():
        give(v_acc, got_line.at[in_line], 0, (c + 1, m))

    staggered([(number, opened[number]) for number in parked], 1, finish, park)

    @pl.when(odd)
    def _():
        got_line[in_line] = v_acc[...]
        settle(got_line.at[pl.ds(0, 15)], sum_recv.at[0])
        total[...] = jnp.sum(got_line[...], axis=0)
        for j in FAR_FIRST:
            give(total, got_plane.at[in_plane], 1, plane(j, 0))
            give(total, got_plane.at[in_plane], 1, plane(j, 1))
        give(total, got_plane.at[in_plane], 1, (c - 1, m))
        got_plane[in_plane] = total[...]


    for copy in backs:
        copy.wait_recv()
    for k, out in enumerate((att_out, dq_out, dh_out)):
        for at in range(0, columns, PAIR):
            cols = slice(at, at + PAIR)
            kept = done[0, k, :, cols]
            handed = done[1, k, :, cols] if at < moved * HEAD else back[(at - moved * HEAD) // PAIR, k]
            out[:ROWS, cols] = jnp.where(first_kept[:, cols], kept, handed)
            out[ROWS:, cols] = jnp.where(first_kept[:, cols], handed, kept)
    for copy in sends + guests + backs:
        copy.wait_send()

    @pl.when(odd)
    def _():
        settle(got_line.at[pl.ds(0, 7)], sum_send.at[0])
        settle(got_plane.at[pl.ds(0, 15)], sum_recv.at[1])
        settle(got_plane.at[pl.ds(0, 15)], sum_send.at[1])
        settle(got_plane, sum_send.at[1])

    @pl.when(jnp.logical_not(odd))
    def _():
        settle(got_line.at[pl.ds(0, 8)], sum_send.at[0])
        settle(got_plane, sum_recv.at[1])

    v = jnp.sum(got_plane[...], axis=0)
    gains_out[0:1, :] = v * gk[...]
    gains_out[1:2, :] = v * gq[...]


def last_kernel(*refs):
    sources, targets, sem = refs[:4], refs[4:8], refs[8]
    stores = [
        pltpu.make_async_copy(src, dst, sem.at[i]) for i, (src, dst) in enumerate(zip(sources, targets))
    ]
    for store in stores:
        store.start()
    for store in stores:
        store.wait()


def per_device(hidden, queries, out_grad, nbrs, query_gain, key_gain, counts, owners):
    rows, columns = hidden.shape
    heads = columns // HEAD
    block = jax.ShapeDtypeStruct((rows, columns), BF16)
    vmem = pl.BlockSpec(memory_space=pltpu.VMEM)
    hbm = pl.BlockSpec(memory_space=pl.ANY)
    dma = pltpu.SemaphoreType.DMA
    gq, gk = query_gain[None], key_gain[None]
    moved = heads // 2
    pairs = (heads - moved) // 2
    results = pl.pallas_call(
        functools.partial(main_kernel, heads),
        out_shape=[pltpu.VMEM((rows, columns), BF16)] * 3 + [pltpu.VMEM((2, HEAD), F32)],
        in_specs=[hbm] * 8,
        out_specs=[vmem, vmem, vmem, vmem],
        scratch_shapes=[
            pltpu.SMEM(counts.shape, jnp.int32),
            pltpu.SMEM(counts.shape, jnp.int32),
            pltpu.VMEM((1, HEAD), F32),
            pltpu.VMEM((1, HEAD), F32),
            pltpu.VMEM((3, rows, columns), BF16),
            pltpu.VMEM((SLOTS, NBR, columns), BF16),
            pltpu.VMEM((SENT_SLOTS, NBR, columns), BF16),
            *[pltpu.VMEM((pairs, 3, ROWS, PAIR), BF16)] * 4,
            pltpu.VMEM((2, 3, ROWS, columns), BF16),
            pltpu.VMEM((1, HEAD), F32),
            pltpu.VMEM((1, HEAD), F32),
            pltpu.VMEM((16, 1, HEAD), F32),
            pltpu.VMEM((16, 1, HEAD), F32),
            dma((4,)), dma((3,)), dma((2,)), dma, dma((moved,)), dma((moved,)), dma((pairs,)), dma((pairs,)),
            dma((pairs,)), dma((pairs,)), dma((2,)), dma((2,)),
        ],
        compiler_params=pltpu.CompilerParams(
            collective_id=0, has_side_effects=True, vmem_limit_bytes=VMEM_LIMIT
        ),
    )(counts, owners, hidden, queries, out_grad, nbrs, gq, gk)
    return pl.pallas_call(
        last_kernel,
        out_shape=[block, block, block, jax.ShapeDtypeStruct((2, HEAD), F32)],
        in_specs=[vmem] * 4,
        out_specs=[hbm] * 4,
        scratch_shapes=[dma((4,))],
        compiler_params=pltpu.CompilerParams(vmem_limit_bytes=8 * 1024 * 1024),
    )(*results)


def solution(mesh):
    in_specs = (
        P("ctx", "mp"),
        P("ctx", "mp"),
        P("ctx", "mp"),
        P("ctx", None, None, "mp"),
        P(),
        P(),
        P(),
        P(),
    )
    out_specs = (P("ctx", "mp"), P("ctx", "mp"), P("ctx", "mp"), P())
    return jax.shard_map(
        per_device, mesh=mesh, in_specs=in_specs, out_specs=out_specs, check_vma=False
    )
```

```python
import functools
import math

import jax
import jax.numpy as jnp
from jax import lax
from jax.experimental import pallas as pl
from jax.experimental.pallas import tpu as pltpu
from jax.sharding import PartitionSpec as P

HEAD = 128
ROWS = 64
NBR = 128
SLOTS = 4
SENT_SLOTS = 2
PAIR = 2 * HEAD
EPSILON = 1e-06
SCALE = 1.0 / math.sqrt(HEAD)
LOG2E = math.log2(math.e)
FAR_FIRST = (10, 6, 9, 11, 14, 2, 8, 5, 7, 13, 15, 1, 3, 4, 12)
MESH = pl.DeviceIdType.MESH
VMEM_LIMIT = 63 * 1024 * 1024
BF16 = jnp.bfloat16
F32 = jnp.float32


def mm(a, b):
    return lax.dot_general(a, b, (((1,), (0,)), ((), ())), preferred_element_type=F32)


def mm_nt(a, b):
    return lax.dot_general(a, b, (((1,), (1,)), ((), ())), preferred_element_type=F32)


def mm_tn(a, b):
    return lax.dot_general(a, b, (((0,), (0,)), ((), ())), preferred_element_type=F32)


def row_norm(value):
    wide = value.astype(F32)
    factor = lax.rsqrt(jnp.mean(wide * wide, axis=1, keepdims=True) + EPSILON)
    return wide * factor, factor


def over_rows(value, row):
    k = row.shape[0]
    return (value.reshape(-1, k, value.shape[1]) * row[None]).reshape(value.shape)


def unit(get_x, get_rows, x_first, gain, live, result):
    eye = (
        lax.broadcasted_iota(jnp.int32, (HEAD, HEAD), 0)
        == lax.broadcasted_iota(jnp.int32, (HEAD, HEAD), 1)
    ).astype(BF16)
    ones = jnp.ones((16, HEAD), BF16)
    root = math.sqrt(HEAD)

    def from_x(x):
        xt = jnp.transpose(x)
        return x, xt, lax.rsqrt(mm(ones, xt * xt) + HEAD * EPSILON)

    def from_rows(h, q, g):
        hf, qf = h.astype(F32), q.astype(F32)
        rh = lax.rsqrt(jnp.sum(hf * hf, axis=1, keepdims=True) + HEAD * EPSILON)
        rq = lax.rsqrt(jnp.sum(qf * qf, axis=1, keepdims=True) + HEAD * EPSILON)
        hn, qn = hf * rh, qf * rq
        qg = jnp.concatenate([qn.astype(BF16), g], axis=0)
        mix = jnp.concatenate([eye, jnp.transpose(h)], axis=1)
        back_mix = jnp.concatenate([jnp.transpose(qg), eye], axis=1)
        return h, rh, rq, hn, qn, qg, mix, back_mix, (hn * gain).astype(BF16)

    if x_first:
        x, xt, rx = from_x(get_x())
        yield "pre"
        h, rh, rq, hn, qn, qg, mix, back_mix, ek = from_rows(*get_rows())
    else:
        h, rh, rq, hn, qn, qg, mix, back_mix, ek = from_rows(*get_rows())
        yield "pre"
        x, xt, rx = from_x(get_x())
    yield
    s = mm(ek, xt)
    yield
    p = jnp.exp2(over_rows(s, rx[:8] * (root * LOG2E)))
    wb = (p * (1.0 / jnp.sum(p, axis=0, keepdims=True))).astype(BF16)
    yield
    eb = mm(mix, jnp.concatenate([xt, wb], axis=0)).astype(BF16)
    yield
    both = mm(qg, eb)
    re = lax.rsqrt(mm(ones, eb * eb) + HEAD * EPSILON)
    yield
    t, da = both[:ROWS], both[ROWS:]
    p = jnp.exp2(over_rows(t, re[:8] * (root * LOG2E)))
    p = jnp.concatenate([p[:, :NBR], p[:, NBR:] * live[:, NBR:]], axis=1)
    inv = 1.0 / jnp.sum(p, axis=1, keepdims=True)
    shift = jnp.sum(p * da, axis=1, keepdims=True) * inv
    ab = (p * inv).astype(BF16)
    dtf = over_rows(p * inv * (da - shift), re[:8] * root)
    dt = dtf.astype(BF16)
    ta = jnp.concatenate([dt, ab], axis=0)
    yield
    c = jnp.sum(dtf * t, axis=0, keepdims=True) * (re * re)
    ec = over_rows(eb, (-c).astype(BF16))
    yield
    deb = mm(back_mix, jnp.concatenate([ta, ec], axis=0)).astype(BF16)
    yield
    dw = mm(h, deb)
    yield
    ds = wb * (dw - jnp.sum(wb.astype(F32) * dw, axis=0, keepdims=True)).astype(BF16)
    ux = mm(over_rows(ds, (rx * root).astype(BF16)), x)
    yield
    u = ux * hn
    result.append(jnp.sum(u, axis=0, keepdims=True))
    yield "v"
    dqo = mm_nt(ta, eb)
    dh = mm_nt(wb, deb)
    yield
    dqn = dqo[:ROWS]
    dq = rq * (dqn - qn * jnp.sum(dqn * qn, axis=1, keepdims=True))
    dh = dh + rh * (ux * gain - hn * jnp.sum(u * gain, axis=1, keepdims=True))
    result.append((dqo[ROWS:].astype(BF16), dq.astype(BF16), dh.astype(BF16)))


def staggered(waiting, every, finish, later, at_once=1):
    waiting, running, tick = list(waiting), [], 0
    while waiting or running:
        if tick % every == 0:
            running, waiting = running + waiting[:at_once], waiting[at_once:]
        still = []
        for number, steps in running:
            if not hasattr(steps, "send"):
                steps = steps()
            mark = next(steps, "end")
            if mark == "end":
                finish(number)
            elif mark in ("pre", "v") and later(number, mark):
                continue
            else:
                still.append((number, steps))
        running = still
        tick += 1


def main_kernel(
    heads, counts_in, owners_in, hidden, queries, out_grad, nbrs, gq_in, gk_in,
    att_out, dq_out, dh_out, gains_out,
    counts, owners, gq, gk, rows_buf, kept_buf, sent_buf, stage, guest, guest_out, back, done, v_acc, total, got_line, got_plane,
    small_sem, in_sem, kept_sem, own_sem, send_sem, recv_sem, guest_send, guest_recv, back_send, back_recv, sum_send, sum_recv,
):
    c = lax.axis_index("ctx")
    m = lax.axis_index("mp")
    n = lax.axis_size("ctx")
    following, preceding = lax.rem(c + 1, n), lax.rem(c + n - 1, n)
    core, z, y = lax.rem(c, 2), lax.rem(lax.div(c, 2), 8), lax.div(c, 16)
    odd = core == 1
    columns = heads * HEAD
    moved = heads // 2
    pairs = (heads - moved) // 2

    line_at = [y * 16 + lax.rem(z + j, 8) * 2 for j in range(8)]
    y_at = [lax.rem(y + j, 4) * 16 + z * 2 for j in range(4)]
    m_at = [lax.rem(m + j, 4) for j in range(4)]

    def line(j, other):
        return (line_at[j] + other, m)

    def plane(j, other):
        return (y_at[j // 4] + other, m_at[j % 4])

    barrier = pltpu.get_barrier_semaphore()

    def greet(device):
        pl.semaphore_signal(barrier, inc=1, device_id=device, device_id_type=MESH)

    @pl.when(odd)
    def _():
        for j in (4, 3, 5, 2, 6, 1, 7):
            greet(line(j, 0))
            greet(line(j, 1))

    for j in FAR_FIRST:
        greet(plane(j, 1))
    greet((following, m))
    greet((preceding, m))
    greet((c + 1 - 2 * core, m))

    small = [
        pltpu.make_async_copy(src, dst, small_sem.at[i])
        for i, (src, dst) in enumerate(((owners_in, owners), (counts_in, counts), (gq_in, gq), (gk_in, gk)))
    ]
    for load in small:
        load.start()
    loads = [
        pltpu.make_async_copy(src, rows_buf.at[i], in_sem.at[i])
        for i, src in enumerate((hidden, queries, out_grad))
    ]
    for load in loads:
        load.start()
    half = columns // 2
    kept_loads = [
        pltpu.make_async_copy(
            nbrs.at[1, :, :, pl.ds(i * half, half)], kept_buf.at[:, :, pl.ds(i * half, half)], kept_sem.at[i]
        )
        for i in range(2)
    ]
    own_cols = pl.ds(moved * HEAD, columns - moved * HEAD)
    own_load = pltpu.make_async_copy(
        nbrs.at[0, pl.ds(0, SENT_SLOTS), :, own_cols], sent_buf.at[:, :, own_cols], own_sem
    )
    for load in kept_loads:
        load.start()

    own_load.start()
    for load in small:
        load.wait()
    gain = gq[...] * gk[...]
    lanes = lax.broadcasted_iota(jnp.int32, (1, SLOTS * NBR), 1)

    def masks(device):
        first_kept = jnp.full(lanes.shape, owners[2 * device], jnp.int32) == device
        first = jnp.full(lanes.shape, counts[2 * device] * NBR, jnp.int32)
        second = jnp.full(lanes.shape, counts[2 * device + 1] * NBR, jnp.int32)
        kept = jnp.where(lanes < jnp.where(first_kept, first, second), 1.0, 0.0)
        handed = jnp.where(lanes < jnp.where(first_kept, second, first), 1.0, 0.0)
        return kept, handed[:, : SENT_SLOTS * NBR]

    live, live_sent = masks(c)
    live_guest = masks(preceding)[1]
    for load in loads:
        load.wait()
    first_kept = jnp.full((ROWS, columns), owners[2 * c], jnp.int32) == c
    for k in range(3):
        top, bottom = rows_buf[k, :ROWS], rows_buf[k, ROWS:]
        rows_buf[k, :ROWS] = jnp.where(first_kept, top, bottom)
        handed = jnp.where(first_kept, bottom, top)
        rows_buf[k, ROWS:] = handed
        for p in range(pairs):
            at = moved * HEAD + p * PAIR
            stage[p, k] = handed[:, at : at + PAIR]
    @pl.when(odd)
    def _():
        pl.semaphore_wait(barrier, 2 + 7 + 31)

    @pl.when(jnp.logical_not(odd))
    def _():
        pl.semaphore_wait(barrier, 2 + 8)

    sends = [
        pltpu.make_async_remote_copy(
            src_ref=nbrs.at[0, pl.ds(0, SENT_SLOTS), :, pl.ds(i * HEAD, HEAD)],
            dst_ref=sent_buf.at[:, :, pl.ds(i * HEAD, HEAD)],
            send_sem=send_sem.at[i], recv_sem=recv_sem.at[i],
            device_id=(preceding, m), device_id_type=MESH,
        )
        for i in range(moved)
    ]
    for copy in sends:
        copy.start()
    guests = [
        pltpu.make_async_remote_copy(
            src_ref=stage.at[p], dst_ref=guest.at[p], send_sem=guest_send.at[p], recv_sem=guest_recv.at[p],
            device_id=(following, m), device_id_type=MESH,
        )
        for p in range(pairs)
    ]
    backs = [
        pltpu.make_async_remote_copy(
            src_ref=guest_out.at[p], dst_ref=back.at[p], send_sem=back_send.at[p], recv_sem=back_recv.at[p],
            device_id=(preceding, m), device_id_type=MESH,
        )
        for p in range(pairs)
    ]

    for copy in guests:
        copy.start()
    for load in kept_loads:
        load.wait()


    def block(buf, i):
        return buf[:, :, pl.ds(i * HEAD, HEAD)].reshape(-1, HEAD)

    def own_rows(first, i):
        return [rows_buf[k, first : first + ROWS, pl.ds(i * HEAD, HEAD)] for k in range(3)]

    def kept_unit(i, result):
        return unit(lambda: block(kept_buf, i), lambda: own_rows(0, i), False, gain, live, result)

    def sent_unit(i, result):
        def arrived():
            if i % 2 == 0:
                sends[i].wait_recv()
                sends[i + 1].wait_recv()
            return block(sent_buf, i)

        return unit(arrived, lambda: own_rows(ROWS, i), False, gain, live_sent, result)

    def guest_unit(i, result):
        p, r = divmod(i - moved, 2)

        def arrived():
            if r == 0:
                guests[p].wait_recv()
            return [guest[p, k, :, r * HEAD : (r + 1) * HEAD] for k in range(3)]

        return unit(lambda: block(sent_buf, i), arrived, True, gain, live_guest, result)

    order = [(0, i) for i in range(heads)]
    for p in range(pairs):
        order += [(2, moved + 2 * p), (2, moved + 2 * p + 1), (1, 2 * p), (1, 2 * p + 1)]
    results = [[] for _ in order]
    parked = []

    def open_unit(number):
        kind, i = order[number]
        return (kept_unit, sent_unit, guest_unit)[kind](i, results[number])

    makers = [(number, functools.partial(open_unit, number)) for number in range(len(order))]

    def finish(number):
        kind, i = order[number]
        for k in range(3):
            value = results[number][1][k]
            if kind == 2:
                p, r = divmod(i - moved, 2)
                guest_out[p, k, :, r * HEAD : (r + 1) * HEAD] = value
            else:
                done[kind, k, :, pl.ds(i * HEAD, HEAD)] = value
        if kind == 2 and r == 1:
            backs[p].start()

    opened = {}

    def begin(number):
        opened[number] = open_unit(number)
        return opened[number]

    makers = [(number, functools.partial(begin, number)) for number in range(len(order))]
    ready = []

    def hold(number, mark):
        held = number >= heads and mark == "pre"
        if held:
            ready.append((number, opened[number]))
        return held

    def park(number, mark):
        if mark == "v":
            parked.append(number)
        return mark == "v"

    own_load.wait()
    staggered(makers, 1, finish, hold, 2)
    staggered(ready, 4, finish, park, 4)
    v_acc[...] = sum(result[0] for result in results)

    def give(src, slot, phase, device):
        pltpu.make_async_remote_copy(
            src_ref=src, dst_ref=slot, send_sem=sum_send.at[phase], recv_sem=sum_recv.at[phase],
            device_id=device, device_id_type=MESH,
        ).start()

    def settle(ref, sem):
        pltpu.make_async_copy(ref, ref, sem).wait()

    in_line, in_plane = z * 2 + core, y * 4 + m
    for j in (4, 3, 5, 2, 6, 1, 7):
        give(v_acc, got_line.at[in_line], 0, line(j, 1))

    @pl.when(jnp.logical_not(odd))
    def _():
        give(v_acc, got_line.at[in_line], 0, (c + 1, m))

    staggered([(number, opened[number]) for number in parked], 1, finish, park)

    @pl.when(odd)
    def _():
        got_line[in_line] = v_acc[...]
        settle(got_line.at[pl.ds(0, 15)], sum_recv.at[0])
        total[...] = jnp.sum(got_line[...], axis=0)
        for j in FAR_FIRST:
            give(total, got_plane.at[in_plane], 1, plane(j, 0))
            give(total, got_plane.at[in_plane], 1, plane(j, 1))
        give(total, got_plane.at[in_plane], 1, (c - 1, m))
        got_plane[in_plane] = total[...]


    for copy in backs:
        copy.wait_recv()
    for k, out in enumerate((att_out, dq_out, dh_out)):
        for at in range(0, columns, PAIR):
            cols = slice(at, at + PAIR)
            kept = done[0, k, :, cols]
            handed = done[1, k, :, cols] if at < moved * HEAD else back[(at - moved * HEAD) // PAIR, k]
            out[:ROWS, cols] = jnp.where(first_kept[:, cols], kept, handed)
            out[ROWS:, cols] = jnp.where(first_kept[:, cols], handed, kept)
    for copy in sends + guests + backs:
        copy.wait_send()

    @pl.when(odd)
    def _():
        settle(got_line.at[pl.ds(0, 7)], sum_send.at[0])
        settle(got_plane.at[pl.ds(0, 15)], sum_recv.at[1])
        settle(got_plane.at[pl.ds(0, 15)], sum_send.at[1])
        settle(got_plane, sum_send.at[1])

    @pl.when(jnp.logical_not(odd))
    def _():
        settle(got_line.at[pl.ds(0, 8)], sum_send.at[0])
        settle(got_plane, sum_recv.at[1])

    v = jnp.sum(got_plane[...], axis=0)
    gains_out[0:1, :] = v * gk[...]
    gains_out[1:2, :] = v * gq[...]


def last_kernel(*refs):
    sources, targets, sem = refs[:4], refs[4:8], refs[8]
    stores = [
        pltpu.make_async_copy(src, dst, sem.at[i]) for i, (src, dst) in enumerate(zip(sources, targets))
    ]
    for store in stores:
        store.start()
    for store in stores:
        store.wait()


def per_device(hidden, queries, out_grad, nbrs, query_gain, key_gain, counts, owners):
    rows, columns = hidden.shape
    heads = columns // HEAD
    block = jax.ShapeDtypeStruct((rows, columns), BF16)
    vmem = pl.BlockSpec(memory_space=pltpu.VMEM)
    hbm = pl.BlockSpec(memory_space=pl.ANY)
    dma = pltpu.SemaphoreType.DMA
    gq, gk = query_gain[None], key_gain[None]
    moved = heads // 2
    pairs = (heads - moved) // 2
    results = pl.pallas_call(
        functools.partial(main_kernel, heads),
        out_shape=[pltpu.VMEM((rows, columns), BF16)] * 3 + [pltpu.VMEM((2, HEAD), F32)],
        in_specs=[hbm] * 8,
        out_specs=[vmem, vmem, vmem, vmem],
        scratch_shapes=[
            pltpu.SMEM(counts.shape, jnp.int32),
            pltpu.SMEM(counts.shape, jnp.int32),
            pltpu.VMEM((1, HEAD), F32),
            pltpu.VMEM((1, HEAD), F32),
            pltpu.VMEM((3, rows, columns), BF16),
            pltpu.VMEM((SLOTS, NBR, columns), BF16),
            pltpu.VMEM((SENT_SLOTS, NBR, columns), BF16),
            *[pltpu.VMEM((pairs, 3, ROWS, PAIR), BF16)] * 4,
            pltpu.VMEM((2, 3, ROWS, columns), BF16),
            pltpu.VMEM((1, HEAD), F32),
            pltpu.VMEM((1, HEAD), F32),
            pltpu.VMEM((16, 1, HEAD), F32),
            pltpu.VMEM((16, 1, HEAD), F32),
            dma((4,)), dma((3,)), dma((2,)), dma, dma((moved,)), dma((moved,)), dma((pairs,)), dma((pairs,)),
            dma((pairs,)), dma((pairs,)), dma((2,)), dma((2,)),
        ],
        compiler_params=pltpu.CompilerParams(
            collective_id=0, has_side_effects=True, vmem_limit_bytes=VMEM_LIMIT
        ),
    )(counts, owners, hidden, queries, out_grad, nbrs, gq, gk)
    return pl.pallas_call(
        last_kernel,
        out_shape=[block, block, block, jax.ShapeDtypeStruct((2, HEAD), F32)],
        in_specs=[vmem] * 4,
        out_specs=[hbm] * 4,
        scratch_shapes=[dma((4,))],
        compiler_params=pltpu.CompilerParams(vmem_limit_bytes=8 * 1024 * 1024),
    )(*results)


def solution(mesh):
    in_specs = (
        P("ctx", "mp"),
        P("ctx", "mp"),
        P("ctx", "mp"),
        P("ctx", None, None, "mp"),
        P(),
        P(),
        P(),
        P(),
    )
    out_specs = (P("ctx", "mp"), P("ctx", "mp"), P("ctx", "mp"), P())
    return jax.shard_map(
        per_device, mesh=mesh, in_specs=in_specs, out_specs=out_specs, check_vma=False
    )
```

```python
import functools
import math

import jax
import jax.numpy as jnp
from jax import lax
from jax.experimental import pallas as pl
from jax.experimental.pallas import tpu as pltpu
from jax.sharding import PartitionSpec as P

HEAD = 128
ROWS = 64
NBR = 128
SLOTS = 4
SENT_SLOTS = 2
PAIR = 2 * HEAD
EPSILON = 1e-06
SCALE = 1.0 / math.sqrt(HEAD)
LOG2E = math.log2(math.e)
FAR_FIRST = (10, 6, 9, 11, 14, 2, 8, 5, 7, 13, 15, 1, 3, 4, 12)
MESH = pl.DeviceIdType.MESH
VMEM_LIMIT = 63 * 1024 * 1024
BF16 = jnp.bfloat16
F32 = jnp.float32


def mm(a, b):
    return lax.dot_general(a, b, (((1,), (0,)), ((), ())), preferred_element_type=F32)


def mm_nt(a, b):
    return lax.dot_general(a, b, (((1,), (1,)), ((), ())), preferred_element_type=F32)


def mm_tn(a, b):
    return lax.dot_general(a, b, (((0,), (0,)), ((), ())), preferred_element_type=F32)


def row_norm(value):
    wide = value.astype(F32)
    factor = lax.rsqrt(jnp.mean(wide * wide, axis=1, keepdims=True) + EPSILON)
    return wide * factor, factor


def over_rows(value, row):
    k = row.shape[0]
    return (value.reshape(-1, k, value.shape[1]) * row[None]).reshape(value.shape)


def unit(get_x, get_rows, x_first, gain, live, result):
    eye = (
        lax.broadcasted_iota(jnp.int32, (HEAD, HEAD), 0)
        == lax.broadcasted_iota(jnp.int32, (HEAD, HEAD), 1)
    ).astype(BF16)
    ones = jnp.ones((16, HEAD), BF16)
    root = math.sqrt(HEAD)

    def from_x(x):
        xt = jnp.transpose(x)
        return x, xt, lax.rsqrt(mm(ones, xt * xt) + HEAD * EPSILON)

    def from_rows(h, q, g):
        hf, qf = h.astype(F32), q.astype(F32)
        rh = lax.rsqrt(jnp.sum(hf * hf, axis=1, keepdims=True) + HEAD * EPSILON)
        rq = lax.rsqrt(jnp.sum(qf * qf, axis=1, keepdims=True) + HEAD * EPSILON)
        hn, qn = hf * rh, qf * rq
        qg = jnp.concatenate([qn.astype(BF16), g], axis=0)
        mix = jnp.concatenate([eye, jnp.transpose(h)], axis=1)
        back_mix = jnp.concatenate([jnp.transpose(qg), eye], axis=1)
        return h, rh, rq, hn, qn, qg, mix, back_mix, (hn * gain).astype(BF16)

    if x_first:
        x, xt, rx = from_x(get_x())
        yield "pre"
        h, rh, rq, hn, qn, qg, mix, back_mix, ek = from_rows(*get_rows())
    else:
        h, rh, rq, hn, qn, qg, mix, back_mix, ek = from_rows(*get_rows())
        yield "pre"
        x, xt, rx = from_x(get_x())
    yield
    s = mm(ek, xt)
    yield
    p = jnp.exp2(over_rows(s, rx[:8] * (root * LOG2E)))
    wb = (p * (1.0 / jnp.sum(p, axis=0, keepdims=True))).astype(BF16)
    yield
    eb = mm(mix, jnp.concatenate([xt, wb], axis=0)).astype(BF16)
    yield
    both = mm(qg, eb)
    re = lax.rsqrt(mm(ones, eb * eb) + HEAD * EPSILON)
    yield
    t, da = both[:ROWS], both[ROWS:]
    p = jnp.exp2(over_rows(t, re[:8] * (root * LOG2E)))
    p = jnp.concatenate([p[:, :NBR], p[:, NBR:] * live[:, NBR:]], axis=1)
    inv = 1.0 / jnp.sum(p, axis=1, keepdims=True)
    shift = jnp.sum(p * da, axis=1, keepdims=True) * inv
    ab = (p * inv).astype(BF16)
    dtf = over_rows(p * inv * (da - shift), re[:8] * root)
    dt = dtf.astype(BF16)
    ta = jnp.concatenate([dt, ab], axis=0)
    yield
    c = jnp.sum(dtf * t, axis=0, keepdims=True) * (re * re)
    ec = over_rows(eb, (-c).astype(BF16))
    yield
    deb = mm(back_mix, jnp.concatenate([ta, ec], axis=0)).astype(BF16)
    yield
    dw = mm(h, deb)
    yield
    ds = wb * (dw - jnp.sum(wb.astype(F32) * dw, axis=0, keepdims=True)).astype(BF16)
    ux = mm(over_rows(ds, (rx * root).astype(BF16)), x)
    yield
    u = ux * hn
    result.append(jnp.sum(u, axis=0, keepdims=True))
    yield "v"
    dqo = mm_nt(ta, eb)
    dh = mm_nt(wb, deb)
    yield
    dqn = dqo[:ROWS]
    dq = rq * (dqn - qn * jnp.sum(dqn * qn, axis=1, keepdims=True))
    dh = dh + rh * (ux * gain - hn * jnp.sum(u * gain, axis=1, keepdims=True))
    result.append((dqo[ROWS:].astype(BF16), dq.astype(BF16), dh.astype(BF16)))


def staggered(waiting, every, finish, later, at_once=1):
    waiting, running, tick = list(waiting), [], 0
    while waiting or running:
        if tick % every == 0:
            running, waiting = running + waiting[:at_once], waiting[at_once:]
        still = []
        for number, steps in running:
            if not hasattr(steps, "send"):
                steps = steps()
            mark = next(steps, "end")
            if mark == "end":
                finish(number)
            elif mark in ("pre", "v") and later(number, mark):
                continue
            else:
                still.append((number, steps))
        running = still
        tick += 1


def main_kernel(
    heads, counts_in, owners_in, hidden, queries, out_grad, nbrs, gq_in, gk_in,
    att_out, dq_out, dh_out, gains_out,
    counts, owners, gq, gk, rows_buf, kept_buf, sent_buf, stage, guest, guest_out, back, done, v_acc, total, got_line, got_plane,
    small_sem, in_sem, kept_sem, own_sem, send_sem, recv_sem, guest_send, guest_recv, back_send, back_recv, sum_send, sum_recv,
):
    c = lax.axis_index("ctx")
    m = lax.axis_index("mp")
    n = lax.axis_size("ctx")
    following, preceding = lax.rem(c + 1, n), lax.rem(c + n - 1, n)
    core, z, y = lax.rem(c, 2), lax.rem(lax.div(c, 2), 8), lax.div(c, 16)
    odd = core == 1
    columns = heads * HEAD
    moved = heads // 2
    pairs = (heads - moved) // 2

    line_at = [y * 16 + lax.rem(z + j, 8) * 2 for j in range(8)]
    y_at = [lax.rem(y + j, 4) * 16 + z * 2 for j in range(4)]
    m_at = [lax.rem(m + j, 4) for j in range(4)]

    def line(j, other):
        return (line_at[j] + other, m)

    def plane(j, other):
        return (y_at[j // 4] + other, m_at[j % 4])

    barrier = pltpu.get_barrier_semaphore()

    def greet(device):
        pl.semaphore_signal(barrier, inc=1, device_id=device, device_id_type=MESH)

    @pl.when(odd)
    def _():
        for j in (4, 3, 5, 2, 6, 1, 7):
            greet(line(j, 0))
            greet(line(j, 1))

    for j in FAR_FIRST:
        greet(plane(j, 1))
    greet((following, m))
    greet((preceding, m))
    greet((c + 1 - 2 * core, m))

    small = [
        pltpu.make_async_copy(src, dst, small_sem.at[i])
        for i, (src, dst) in enumerate(((owners_in, owners), (counts_in, counts), (gq_in, gq), (gk_in, gk)))
    ]
    for load in small:
        load.start()
    loads = [
        pltpu.make_async_copy(src, rows_buf.at[i], in_sem.at[i])
        for i, src in enumerate((hidden, queries, out_grad))
    ]
    for load in loads:
        load.start()
    half = columns // 2
    kept_loads = [
        pltpu.make_async_copy(
            nbrs.at[1, :, :, pl.ds(i * half, half)], kept_buf.at[:, :, pl.ds(i * half, half)], kept_sem.at[i]
        )
        for i in range(2)
    ]
    own_cols = pl.ds(moved * HEAD, columns - moved * HEAD)
    own_load = pltpu.make_async_copy(
        nbrs.at[0, pl.ds(0, SENT_SLOTS), :, own_cols], sent_buf.at[:, :, own_cols], own_sem
    )
    for load in kept_loads:
        load.start()

    own_load.start()
    for load in small:
        load.wait()
    gain = gq[...] * gk[...]
    lanes = lax.broadcasted_iota(jnp.int32, (1, SLOTS * NBR), 1)

    def masks(device):
        first_kept = jnp.full(lanes.shape, owners[2 * device], jnp.int32) == device
        first = jnp.full(lanes.shape, counts[2 * device] * NBR, jnp.int32)
        second = jnp.full(lanes.shape, counts[2 * device + 1] * NBR, jnp.int32)
        kept = jnp.where(lanes < jnp.where(first_kept, first, second), 1.0, 0.0)
        handed = jnp.where(lanes < jnp.where(first_kept, second, first), 1.0, 0.0)
        return kept, handed[:, : SENT_SLOTS * NBR]

    live, live_sent = masks(c)
    live_guest = masks(preceding)[1]
    for load in loads:
        load.wait()
    first_kept = jnp.full((ROWS, columns), owners[2 * c], jnp.int32) == c
    for k in range(3):
        top, bottom = rows_buf[k, :ROWS], rows_buf[k, ROWS:]
        rows_buf[k, :ROWS] = jnp.where(first_kept, top, bottom)
        handed = jnp.where(first_kept, bottom, top)
        rows_buf[k, ROWS:] = handed
        for p in range(pairs):
            at = moved * HEAD + p * PAIR
            stage[p, k] = handed[:, at : at + PAIR]
    @pl.when(odd)
    def _():
        pl.semaphore_wait(barrier, 2 + 7 + 31)

    @pl.when(jnp.logical_not(odd))
    def _():
        pl.semaphore_wait(barrier, 2 + 8)

    sends = [
        pltpu.make_async_remote_copy(
            src_ref=nbrs.at[0, pl.ds(0, SENT_SLOTS), :, pl.ds(i * HEAD, HEAD)],
            dst_ref=sent_buf.at[:, :, pl.ds(i * HEAD, HEAD)],
            send_sem=send_sem.at[i], recv_sem=recv_sem.at[i],
            device_id=(preceding, m), device_id_type=MESH,
        )
        for i in range(moved)
    ]
    for copy in sends:
        copy.start()
    guests = [
        pltpu.make_async_remote_copy(
            src_ref=stage.at[p], dst_ref=guest.at[p], send_sem=guest_send.at[p], recv_sem=guest_recv.at[p],
            device_id=(following, m), device_id_type=MESH,
        )
        for p in range(pairs)
    ]
    backs = [
        pltpu.make_async_remote_copy(
            src_ref=guest_out.at[p], dst_ref=back.at[p], send_sem=back_send.at[p], recv_sem=back_recv.at[p],
            device_id=(preceding, m), device_id_type=MESH,
        )
        for p in range(pairs)
    ]

    for copy in guests:
        copy.start()
    for load in kept_loads:
        load.wait()


    def block(buf, i):
        return buf[:, :, pl.ds(i * HEAD, HEAD)].reshape(-1, HEAD)

    def own_rows(first, i):
        return [rows_buf[k, first : first + ROWS, pl.ds(i * HEAD, HEAD)] for k in range(3)]

    def kept_unit(i, result):
        return unit(lambda: block(kept_buf, i), lambda: own_rows(0, i), False, gain, live, result)

    def arrive(p):
        guests[p].wait_recv()
        for i in range(2 * p, 2 * p + 2):
            sends[i].wait_recv()

    def sent_unit(i, result):
        return unit(lambda: block(sent_buf, i), lambda: own_rows(ROWS, i), False, gain, live_sent, result)

    def guest_unit(i, result):
        p, r = divmod(i - moved, 2)

        def arrived():
            if r == 0:
                arrive(p)
            return [guest[p, k, :, r * HEAD : (r + 1) * HEAD] for k in range(3)]

        return unit(lambda: block(sent_buf, i), arrived, True, gain, live_guest, result)

    order = [(0, i) for i in range(heads)]
    for p in range(pairs):
        order += [(2, moved + 2 * p), (2, moved + 2 * p + 1), (1, 2 * p), (1, 2 * p + 1)]
    results = [[] for _ in order]
    parked = []

    def open_unit(number):
        kind, i = order[number]
        return (kept_unit, sent_unit, guest_unit)[kind](i, results[number])

    makers = [(number, functools.partial(open_unit, number)) for number in range(len(order))]

    def finish(number):
        kind, i = order[number]
        for k in range(3):
            value = results[number][1][k]
            if kind == 2:
                p, r = divmod(i - moved, 2)
                guest_out[p, k, :, r * HEAD : (r + 1) * HEAD] = value
            else:
                done[kind, k, :, pl.ds(i * HEAD, HEAD)] = value
        if kind == 2 and r == 1:
            backs[p].start()

    opened = {}

    def begin(number):
        opened[number] = open_unit(number)
        return opened[number]

    makers = [(number, functools.partial(begin, number)) for number in range(len(order))]
    ready = []

    def hold(number, mark):
        held = number >= heads and mark == "pre"
        if held:
            ready.append((number, opened[number]))
        return held

    def park(number, mark):
        if mark == "v":
            parked.append(number)
        return mark == "v"

    own_load.wait()
    staggered(makers, 2, finish, hold, 4)
    staggered(ready, 4, finish, park, 4)
    v_acc[...] = sum(result[0] for result in results)

    def give(src, slot, phase, device):
        pltpu.make_async_remote_copy(
            src_ref=src, dst_ref=slot, send_sem=sum_send.at[phase], recv_sem=sum_recv.at[phase],
            device_id=device, device_id_type=MESH,
        ).start()

    def settle(ref, sem):
        pltpu.make_async_copy(ref, ref, sem).wait()

    in_line, in_plane = z * 2 + core, y * 4 + m
    for j in (4, 3, 5, 2, 6, 1, 7):
        give(v_acc, got_line.at[in_line], 0, line(j, 1))

    @pl.when(jnp.logical_not(odd))
    def _():
        give(v_acc, got_line.at[in_line], 0, (c + 1, m))

    staggered([(number, opened[number]) for number in parked], 1, finish, park)

    @pl.when(odd)
    def _():
        got_line[in_line] = v_acc[...]
        settle(got_line.at[pl.ds(0, 15)], sum_recv.at[0])
        total[...] = jnp.sum(got_line[...], axis=0)
        for j in FAR_FIRST:
            give(total, got_plane.at[in_plane], 1, plane(j, 0))
            give(total, got_plane.at[in_plane], 1, plane(j, 1))
        give(total, got_plane.at[in_plane], 1, (c - 1, m))
        got_plane[in_plane] = total[...]


    for copy in backs:
        copy.wait_recv()
    for k, out in enumerate((att_out, dq_out, dh_out)):
        for at in range(0, columns, PAIR):
            cols = slice(at, at + PAIR)
            kept = done[0, k, :, cols]
            handed = done[1, k, :, cols] if at < moved * HEAD else back[(at - moved * HEAD) // PAIR, k]
            out[:ROWS, cols] = jnp.where(first_kept[:, cols], kept, handed)
            out[ROWS:, cols] = jnp.where(first_kept[:, cols], handed, kept)
    for copy in sends + guests + backs:
        copy.wait_send()

    @pl.when(odd)
    def _():
        settle(got_line.at[pl.ds(0, 7)], sum_send.at[0])
        settle(got_plane.at[pl.ds(0, 15)], sum_recv.at[1])
        settle(got_plane.at[pl.ds(0, 15)], sum_send.at[1])
        settle(got_plane, sum_send.at[1])

    @pl.when(jnp.logical_not(odd))
    def _():
        settle(got_line.at[pl.ds(0, 8)], sum_send.at[0])
        settle(got_plane, sum_recv.at[1])

    v = jnp.sum(got_plane[...], axis=0)
    gains_out[0:1, :] = v * gk[...]
    gains_out[1:2, :] = v * gq[...]


def last_kernel(*refs):
    sources, targets, sem = refs[:4], refs[4:8], refs[8]
    stores = [
        pltpu.make_async_copy(src, dst, sem.at[i]) for i, (src, dst) in enumerate(zip(sources, targets))
    ]
    for store in stores:
        store.start()
    for store in stores:
        store.wait()


def per_device(hidden, queries, out_grad, nbrs, query_gain, key_gain, counts, owners):
    rows, columns = hidden.shape
    heads = columns // HEAD
    block = jax.ShapeDtypeStruct((rows, columns), BF16)
    vmem = pl.BlockSpec(memory_space=pltpu.VMEM)
    hbm = pl.BlockSpec(memory_space=pl.ANY)
    dma = pltpu.SemaphoreType.DMA
    gq, gk = query_gain[None], key_gain[None]
    moved = heads // 2
    pairs = (heads - moved) // 2
    results = pl.pallas_call(
        functools.partial(main_kernel, heads),
        out_shape=[pltpu.VMEM((rows, columns), BF16)] * 3 + [pltpu.VMEM((2, HEAD), F32)],
        in_specs=[hbm] * 8,
        out_specs=[vmem, vmem, vmem, vmem],
        scratch_shapes=[
            pltpu.SMEM(counts.shape, jnp.int32),
            pltpu.SMEM(counts.shape, jnp.int32),
            pltpu.VMEM((1, HEAD), F32),
            pltpu.VMEM((1, HEAD), F32),
            pltpu.VMEM((3, rows, columns), BF16),
            pltpu.VMEM((SLOTS, NBR, columns), BF16),
            pltpu.VMEM((SENT_SLOTS, NBR, columns), BF16),
            *[pltpu.VMEM((pairs, 3, ROWS, PAIR), BF16)] * 4,
            pltpu.VMEM((2, 3, ROWS, columns), BF16),
            pltpu.VMEM((1, HEAD), F32),
            pltpu.VMEM((1, HEAD), F32),
            pltpu.VMEM((16, 1, HEAD), F32),
            pltpu.VMEM((16, 1, HEAD), F32),
            dma((4,)), dma((3,)), dma((2,)), dma, dma((moved,)), dma((moved,)), dma((pairs,)), dma((pairs,)),
            dma((pairs,)), dma((pairs,)), dma((2,)), dma((2,)),
        ],
        compiler_params=pltpu.CompilerParams(
            collective_id=0, has_side_effects=True, vmem_limit_bytes=VMEM_LIMIT
        ),
    )(counts, owners, hidden, queries, out_grad, nbrs, gq, gk)
    return pl.pallas_call(
        last_kernel,
        out_shape=[block, block, block, jax.ShapeDtypeStruct((2, HEAD), F32)],
        in_specs=[vmem] * 4,
        out_specs=[hbm] * 4,
        scratch_shapes=[dma((4,))],
        compiler_params=pltpu.CompilerParams(vmem_limit_bytes=8 * 1024 * 1024),
    )(*results)


def solution(mesh):
    in_specs = (
        P("ctx", "mp"),
        P("ctx", "mp"),
        P("ctx", "mp"),
        P("ctx", None, None, "mp"),
        P(),
        P(),
        P(),
        P(),
    )
    out_specs = (P("ctx", "mp"), P("ctx", "mp"), P("ctx", "mp"), P())
    return jax.shard_map(
        per_device, mesh=mesh, in_specs=in_specs, out_specs=out_specs, check_vma=False
    )
```
